32 devices in a mesh: crop: 2 (over core), row: 4 (over y, x), col: 4 (over z).
Axes of the slice: x: 2, y: 2, z: 4, core: 2. Of those that a mesh axis runs over, the one named last changes fastest.
Arguments:
- pair_state: bfloat16 [192, 96, 128], P(('crop', 'row'), 'col'), parts along dimension 0, may hold values from -6 to 6
- token_mask: int32 [192], P('crop'), parts along dimension 0, may hold values from 0 to 1, as said below
- block_pattern: int32 [8, 4], P('crop'), parts along dimension 0, may hold values from 0 to 1, as said below
- triangle_norm: float32 [128], replicated, may hold values from 0.1 to 1.9
- triangle_input: bfloat16 [128, 512], replicated, may hold values from -0.5 to 0.5
- triangle_gate: bfloat16 [128, 128], replicated, may hold values from -0.5 to 0.5
- product_norm: float32 [128], replicated, may hold values from 0.1 to 1.9
- triangle_output: bfloat16 [128, 128], replicated, may hold values from -0.5 to 0.5
- attend_norm: float32 [128], replicated, may hold values from 0.1 to 1.9
- attend_inputs: bfloat16 [128, 384], replicated, may hold values from -4 to 4
- attend_gate: bfloat16 [128, 128], replicated, may hold values from -0.5 to 0.5
- attend_bias: bfloat16 [128, 4], replicated, may hold values from -0.5 to 0.5
- attend_output: bfloat16 [128, 128], replicated, may hold values from -0.5 to 0.5
Outputs:
- pair_output: bfloat16 [192, 96, 128], P(('crop', 'row'), 'col'), parts along dimension 0
The draws below stay inside these ranges and needn't reach their ends.
There are 2 independent parts, one for each index of `crop`. The reference program is written for one: setup_inputs(seed, part) draws one part's arguments, and reference() takes and returns one part's arrays. A program takes and returns all parts, laid end to end along the dimension named above; an argument that names none is the same for every part. Nothing has to cross between parts.
Inputs may be any that keep to these rules, and one draw needn't show every extreme that they name: `token_mask`: 1 on a prefix of 24 or more tokens and 0 after it. `block_pattern`: every row allows its own block and block 0.
All inputs are finite; a program needn't handle non-finite values.
Results may differ from the reference program's by a relative error of at most 0.02.
Values may be sent and summed in bfloat16 or wider, within the bound.
No kernel may reach another device: no remote copies, remote signals or barrier semaphores. Data moves between devices by JAX's collectives and lax.ppermute only.
A program may use at most 64 MiB of HBM per device.

```python
import math
import jax
import jax.numpy as jnp
from jax import lax

C = 128
H = 4
NB = 4
N = 96


def draw_token_mask(key, part):
    length = jax.random.randint(jax.random.fold_in(key, 11), (), N // NB, N + 1)
    positions = jnp.arange(N)
    return (positions < length).astype(jnp.int32)


def draw_block_pattern(key, part):
    random_bits = jax.random.randint(jax.random.fold_in(key, 12), (NB, NB), 0, 2)
    index_grid = jnp.arange(NB)
    forced = (index_grid[:, None] == index_grid[None, :]) | (index_grid[None, :] == 0)
    return jnp.where(forced, 1, random_bits).astype(jnp.int32)


def draw_attend_inputs(key, part):
    drawn = jax.random.normal(jax.random.fold_in(key, 13), (C, 3 * C), jnp.float32) / math.sqrt(C)
    return jnp.clip(drawn, -4.0, 4.0).astype(jnp.bfloat16)


def levels(key, dims, split, least, top_value):
    level, own = 1.0, jax.random.fold_in(key, 6)
    for axis_at, shards_of in split:
        heights = jnp.exp(jax.random.uniform(jax.random.fold_in(own, axis_at), (shards_of,), jnp.float32, least / len(split), top_value / len(split)))
        level = level * jnp.repeat(heights, dims[axis_at] // shards_of).reshape([-1 if axis == axis_at else 1 for axis in range(len(dims))])
    return level


def centred(key, shape, spread, limit, shards=(), dtype=jnp.bfloat16):
    loudness = levels(key, shape, shards, -0.22, 0.18) if shards else 1.0
    entries = jax.random.normal(key, shape, jnp.float32) * spread * loudness
    return jnp.minimum(jnp.maximum(entries, -limit), limit).astype(dtype)


def setup_inputs(seed: int = 0, part: int = 0) -> dict:
    splits = jax.random.split(jax.random.key(seed), 14)
    part_keys = jax.random.split(jax.random.fold_in(splits[13], part), 14)
    pair_state = centred(part_keys[0], (N, N, C), 1.0, 6.0, ((0, 4), (1, 4)))
    token_mask = draw_token_mask(jax.random.fold_in(jax.random.fold_in(splits[13], part), 71), part)
    block_pattern = draw_block_pattern(jax.random.fold_in(jax.random.fold_in(splits[13], part), 71), part)
    triangle_norm = jnp.clip(1.0 + 0.18 * jax.random.normal(splits[3], (C,), jnp.float32), 0.1, 1.9)
    triangle_input = centred(splits[4], (C, 4 * C), C ** -0.5, 0.5)
    triangle_gate = centred(splits[5], (C, C), C ** -0.5, 0.5)
    product_norm = jnp.clip(1.0 + 0.18 * jax.random.normal(splits[6], (C,), jnp.float32), 0.1, 1.9)
    triangle_output = centred(splits[7], (C, C), C ** -0.5, 0.5)
    attend_norm = jnp.clip(1.0 + 0.18 * jax.random.normal(splits[8], (C,), jnp.float32), 0.1, 1.9)
    attend_inputs = draw_attend_inputs(jax.random.fold_in(splits[13], 71), part)
    attend_gate = centred(splits[10], (C, C), C ** -0.5, 0.5)
    attend_bias = centred(splits[11], (C, H), C ** -0.5, 0.5)
    attend_output = centred(splits[12], (C, C), C ** -0.5, 0.5)
    return dict(pair_state=pair_state, token_mask=token_mask, block_pattern=block_pattern, triangle_norm=triangle_norm, triangle_input=triangle_input, triangle_gate=triangle_gate, product_norm=product_norm, triangle_output=triangle_output, attend_norm=attend_norm, attend_inputs=attend_inputs, attend_gate=attend_gate, attend_bias=attend_bias, attend_output=attend_output)


norm_epsilon = 1e-05

def layer_norm(inputs, gain):
    average = lax.optimization_barrier(jnp.mean(inputs, axis=-1, keepdims=True))
    centered = inputs - average
    variance = lax.optimization_barrier(jnp.mean(centered * centered, axis=-1, keepdims=True))
    return centered * lax.rsqrt(variance + norm_epsilon) * gain

def attend_row(pair_row, attend_inputs, attend_gate, head_bias, allowed):
    channels = pair_row.shape[1]
    head_count = head_bias.shape[0]
    head_width = channels // head_count
    combined = jnp.dot(pair_row, attend_inputs, preferred_element_type=jnp.float32)
    queries = combined[:, :channels].astype(jnp.bfloat16).reshape(-1, head_count, head_width)
    key_rows = combined[:, channels:2 * channels].astype(jnp.bfloat16).reshape(-1, head_count, head_width)
    values = combined[:, 2 * channels:].astype(jnp.bfloat16).reshape(-1, head_count, head_width)
    gate_values = jax.nn.sigmoid(jnp.dot(pair_row, attend_gate, preferred_element_type=jnp.float32))
    scores = jnp.einsum('jhd,khd->hjk', queries.astype(jnp.float32), key_rows.astype(jnp.float32)) / math.sqrt(head_width)
    scores = scores + head_bias.astype(jnp.float32)
    scores = jnp.where(allowed[None], scores, -jnp.inf)
    row_max = lax.optimization_barrier(jnp.max(scores, axis=-1, keepdims=True))
    weights = jnp.exp(scores - row_max)
    probabilities = (weights / lax.optimization_barrier(jnp.sum(weights, axis=-1, keepdims=True))).astype(jnp.bfloat16)
    attended = jnp.einsum('hjk,khd->jhd', probabilities.astype(jnp.float32), values.astype(jnp.float32)).reshape(-1, channels)
    return (gate_values * attended).astype(jnp.bfloat16)

def reference(pair_state, token_mask, block_pattern, triangle_norm, triangle_input, triangle_gate, product_norm, triangle_output, attend_norm, attend_inputs, attend_gate, attend_bias, attend_output):
    state_float = pair_state.astype(jnp.float32)
    normed = layer_norm(state_float, triangle_norm).astype(jnp.bfloat16)
    projected = jnp.dot(normed, triangle_input, preferred_element_type=jnp.float32)
    valid_tokens = token_mask.astype(jnp.float32)
    pair_valid = (valid_tokens[:, None] * valid_tokens[None, :])[:, :, None]
    left_factor = (pair_valid * jax.nn.sigmoid(projected[..., :C]) * projected[..., C:2 * C]).astype(jnp.bfloat16)
    right_factor = (pair_valid * jax.nn.sigmoid(projected[..., 2 * C:3 * C]) * projected[..., 3 * C:]).astype(jnp.bfloat16)
    product = jnp.einsum('ikc,jkc->ijc', left_factor.astype(jnp.float32), right_factor.astype(jnp.float32), precision=lax.Precision.HIGHEST)
    product_normed = layer_norm(product, product_norm).astype(jnp.bfloat16)
    gate_values = jax.nn.sigmoid(jnp.dot(normed, triangle_gate, preferred_element_type=jnp.float32))
    middle = (state_float + gate_values * jnp.dot(product_normed, triangle_output, preferred_element_type=jnp.float32)).astype(jnp.bfloat16)
    attend_normed = layer_norm(middle.astype(jnp.float32), attend_norm).astype(jnp.bfloat16)
    head_bias = jnp.transpose(jnp.dot(attend_normed, attend_bias, preferred_element_type=jnp.float32).astype(jnp.bfloat16), (2, 0, 1))
    block_width = N // NB
    pattern_ok = block_pattern[:, None, :, None] > 0
    allowed = jnp.broadcast_to(pattern_ok, (NB, block_width, NB, block_width)).reshape(N, N) & (token_mask[None, :] > 0)
    attended = lax.map(lambda pair_row: attend_row(pair_row, attend_inputs, attend_gate, head_bias, allowed), attend_normed)
    update = jnp.dot(attended, attend_output, preferred_element_type=jnp.float32)
    return (middle.astype(jnp.float32) + update).astype(jnp.bfloat16)
```

```python
import functools
import math

import jax
import jax.numpy as jnp
from jax import lax
from jax.experimental import pallas as pl
from jax.experimental.pallas import tpu as pltpu
from jax.sharding import PartitionSpec as P

norm_epsilon = 1e-05
VMEM = pl.BlockSpec(memory_space=pltpu.VMEM)
PARAMS = pltpu.CompilerParams(vmem_limit_bytes=48 * 1024 * 1024)


def layer_norm(inputs, gain):
    average = jnp.mean(inputs, axis=-1, keepdims=True)
    centered = inputs - average
    variance = jnp.mean(centered * centered, axis=-1, keepdims=True)
    return centered * lax.rsqrt(variance + norm_epsilon) * gain


def dot(left, right):
    return jnp.dot(left, right, preferred_element_type=jnp.float32)


def pair_mask(row_mask, column_mask, rows, columns, row_start, column_start):
    along_rows = row_mask[pl.ds(row_start, rows)]
    along_columns = column_mask[pl.ds(pl.multiple_of(column_start, 8), columns), :]
    return (along_rows * along_columns[None]).reshape(rows * columns, -1)


def own_kernel(rows, columns, state, row_mask, column_mask, gain, w_in, w_gate, left, right, gate):
    channels = state.shape[1]
    row_start = lax.axis_index("row") * rows
    column_start = lax.axis_index("col") * columns
    normed = layer_norm(state[...].astype(jnp.float32), gain[...]).astype(jnp.bfloat16)
    mask = pair_mask(row_mask, column_mask, rows, columns, row_start, column_start)
    part = dot(normed, w_in[:, : 2 * channels])
    value = mask * jax.nn.sigmoid(part[:, :channels]) * part[:, channels:]
    left[...] = value.astype(jnp.bfloat16).astype(jnp.float32)
    part = dot(normed, w_in[:, 2 * channels :])
    value = mask * jax.nn.sigmoid(part[:, :channels]) * part[:, channels:]
    right[...] = value.astype(jnp.bfloat16).astype(jnp.float32)
    gate[...] = jax.nn.sigmoid(dot(normed, w_gate[...]))


def product_kernel(rows, columns, row_devices, column_devices, row_mask, column_mask, gain, w_in, left, right_own, *refs):
    states, refs = refs[: row_devices - 1], refs[row_devices - 1 :]
    outs, right = refs[:column_devices], refs[column_devices]
    channels = left.shape[1]
    size = rows * columns
    split = rows // columns
    row_index, column_index = lax.axis_index("row"), lax.axis_index("col")
    right[pl.ds(0, size), :] = right_own[...]
    for step, state in enumerate(states, 1):
        normed = layer_norm(state[...].astype(jnp.float32), gain[...]).astype(jnp.bfloat16)
        row_start = lax.bitwise_xor(row_index, step) * rows
        mask = pair_mask(row_mask, column_mask, rows, columns, row_start, column_index * columns)
        part = dot(normed, w_in[:, 2 * channels :])
        value = mask * jax.nn.sigmoid(part[:, :channels]) * part[:, channels:]
        right[pl.ds(step * size, size), :] = value.astype(jnp.bfloat16).astype(jnp.float32)
    group = 4 if rows % 4 == 0 else 2
    for step, out in enumerate(outs):
        target = lax.bitwise_xor(column_index, step)
        held = lax.bitwise_xor(row_index, target // split)
        base = held * size + (target % split) * columns * columns

        def block(at, carry, out=out, base=base):
            sums = [jnp.zeros((columns, channels), jnp.float32) for _ in range(group)]
            for k in range(columns):
                factor = right[pl.ds(base + k, columns, stride=columns), :]
                for g in range(group):
                    row = left[pl.ds((at * group + g) * columns + k, 1), :]
                    sums[g] = sums[g] + row * factor
            width = group * columns
            start = pl.multiple_of(at * width, 16)
            out[pl.ds(start, width), :] = jnp.concatenate(sums, 0).astype(jnp.bfloat16)
            return carry

        lax.fori_loop(0, rows // group, block, 0)


def middle_kernel(rows, columns, split, state, gate, product_gain, w_out, attend_gain, w_bias, *refs):
    parts, (middle, attend, bias) = refs[:-3], refs[-3:]
    product = parts[0][...].astype(jnp.float32)
    for part in parts[1:]:
        product = product + part[...].astype(jnp.float32)
    normed = layer_norm(product, product_gain[...]).astype(jnp.bfloat16)
    value = state[...].astype(jnp.float32) + gate[...] * dot(normed, w_out[...])
    rounded = value.astype(jnp.bfloat16)
    middle[...] = rounded
    normed = layer_norm(rounded.astype(jnp.float32), attend_gain[...]).astype(jnp.bfloat16)
    attend[...] = normed
    spread = dot(normed, w_bias[...]).reshape(rows, columns, -1)
    lane = lax.broadcasted_iota(jnp.int32, spread.shape[1:], 1) % columns
    for part in range(split):
        total = jnp.zeros(spread.shape[1:], jnp.float32)
        for j in range(columns):
            total = jnp.where(lane == j, spread[part * columns + j], total)
        bias[part] = total.astype(jnp.bfloat16)


def attend_kernel(rows, columns, heads, split, column_devices, middle, allowed, w_query, w_key_value, w_gate, w_out, *refs):
    tiles, refs = refs[:column_devices], refs[column_devices:]
    biases, refs = refs[:column_devices], refs[column_devices:]
    out, keys, values, queries, gates, bias, gated = refs
    channels = middle.shape[1]
    width = channels // heads
    tokens = columns * column_devices
    row_index, column_index = lax.axis_index("row"), lax.axis_index("col")
    for step, tile in enumerate(tiles):
        part = dot(tile[...], w_key_value[...]).reshape(rows, columns, 2 * channels)
        keys[:, pl.ds(step * columns, columns), :] = part[..., :channels]
        values[:, pl.ds(step * columns, columns), :] = part[..., channels:]
    own = tiles[0][...]
    queries[...] = dot(own, w_query[...])
    gates[...] = jax.nn.sigmoid(dot(own, w_gate[...]))
    for step, piece in enumerate(biases):
        place = lax.bitwise_xor(row_index * split + column_index % split, step)
        place = lax.bitwise_xor(place, column_index)
        bias[pl.ds(pl.multiple_of(place * columns, 8), columns), :] = piece[...].astype(jnp.float32)
    for step in range(column_devices):
        start = pl.multiple_of(lax.bitwise_xor(column_index, step) * columns, 8)
        here = pl.ds(step * columns, columns)
        bias[here, :] = jnp.where(allowed[pl.ds(start, columns), :] > 0, bias[here, :], -1e30)
    added = bias[...].T
    head_of_lane = lax.broadcasted_iota(jnp.int32, (1, channels), 1) // width
    picks = [head_of_lane == h for h in range(heads)]
    scale = 1.0 / math.sqrt(width)
    ones = jnp.ones((tokens, channels), jnp.bfloat16)

    def row(at, carry):
        start = pl.multiple_of(at * columns, 8)
        query = queries[pl.ds(start, columns), :]
        stacked = jnp.concatenate([jnp.where(pick, query, 0.0) for pick in picks], 0).astype(jnp.bfloat16)
        key = keys[at].astype(jnp.bfloat16)
        scores = lax.dot_general(stacked, key, (((1,), (1,)), ((), ())), preferred_element_type=jnp.float32)
        scores = scores * scale + added
        weights = jnp.exp(scores - jnp.max(scores, axis=-1, keepdims=True)).astype(jnp.bfloat16)
        value = jnp.concatenate([values[at].astype(jnp.bfloat16), ones], 1)
        mixed = dot(weights, value)
        mixed = mixed[:, :channels] / mixed[:, channels:]
        total = jnp.zeros((columns, channels), jnp.float32)
        for h, pick in enumerate(picks):
            total = jnp.where(pick, mixed[h * columns : (h + 1) * columns], total)
        gated[pl.ds(start, columns), :] = total * gates[pl.ds(start, columns), :]
        return carry

    lax.fori_loop(0, rows, row, 0, unroll=4)
    update = dot(gated[...].astype(jnp.bfloat16), w_out[...])
    out[...] = (middle[...].astype(jnp.float32) + update).astype(jnp.bfloat16)


def call(kernel, outs, args, scratch=()):
    return pl.pallas_call(
        kernel,
        out_shape=outs,
        in_specs=[VMEM] * len(args),
        out_specs=jax.tree.map(lambda _: VMEM, outs),
        scratch_shapes=scratch,
        compiler_params=PARAMS,
    )(*args)


def exchange(value, axis, step):
    size = lax.axis_size(axis)
    return lax.ppermute(value, axis, [(at, at ^ step) for at in range(size)])


def shards(
    pair_state,
    token_mask,
    block_pattern,
    triangle_norm,
    triangle_input,
    triangle_gate,
    product_norm,
    triangle_output,
    attend_norm,
    attend_inputs,
    attend_gate,
    attend_bias,
    attend_output,
):
    rows, columns, channels = pair_state.shape
    row_devices, column_devices = lax.axis_size("row"), lax.axis_size("col")
    heads = attend_bias.shape[1]
    split = rows // columns
    tokens = columns * column_devices
    size = rows * columns
    row_index, column_index = lax.axis_index("row"), lax.axis_index("col")
    tile = jax.ShapeDtypeStruct((size, channels), jnp.bfloat16)
    wide = jax.ShapeDtypeStruct((size, channels), jnp.float32)
    state = pair_state.reshape(size, channels)
    others = [exchange(state, "row", step) for step in range(1, row_devices)]

    valid = token_mask.astype(jnp.float32)
    row_mask = jnp.broadcast_to(valid[:, None, None], (tokens, 1, channels))
    column_mask = jnp.broadcast_to(valid[:, None], (tokens, channels))
    blocks = block_pattern.shape[0]
    block_width = tokens // blocks
    pattern = jnp.repeat(jnp.repeat(block_pattern, block_width, axis=0), block_width, axis=1)
    pattern = lax.dynamic_slice_in_dim(pattern, column_index * columns, columns, axis=0)
    allowed = ((pattern > 0) & (token_mask[None, :] > 0)).astype(jnp.float32).T
    allowed = jnp.tile(allowed, (1, heads))
    w_bias = jnp.repeat(attend_bias, columns, axis=1)

    left, right, gate = call(
        functools.partial(own_kernel, rows, columns),
        [wide, wide, wide],
        [state, row_mask, column_mask, triangle_norm[None], triangle_input, triangle_gate],
    )
    parts = call(
        functools.partial(product_kernel, rows, columns, row_devices, column_devices),
        [tile] * column_devices,
        [row_mask, column_mask, triangle_norm[None], triangle_input, left, right] + others,
        [pltpu.VMEM((row_devices * size, channels), jnp.float32)],
    )
    parts = [parts[0]] + [exchange(parts[step], "col", step) for step in range(1, column_devices)]
    middle, attend, bias = call(
        functools.partial(middle_kernel, rows, columns, split),
        [tile, tile, jax.ShapeDtypeStruct((split, columns, heads * columns), jnp.bfloat16)],
        [state, gate, product_norm[None], triangle_output, attend_norm[None], w_bias] + parts,
    )
    tiles = [attend] + [exchange(attend, "col", step) for step in range(1, column_devices)]
    biases = []
    for step in range(column_devices):
        piece = bias[0]
        if split > 1:
            piece = lax.dynamic_index_in_dim(bias, lax.bitwise_xor(column_index, step) % split, 0, False)
        pairs = []
        for a in range(row_devices):
            for b in range(column_devices):
                turn = b ^ step
                pairs.append((a * column_devices + b, (turn // split) * column_devices + split * a + turn % split))
        biases.append(lax.ppermute(piece, ("row", "col"), pairs))
    stack = pltpu.VMEM((rows, tokens, channels), jnp.float32)
    flat = pltpu.VMEM((size, channels), jnp.float32)
    result = call(
        functools.partial(attend_kernel, rows, columns, heads, split, column_devices),
        tile,
        [middle, allowed, attend_inputs[:, :channels], attend_inputs[:, channels:], attend_gate, attend_output]
        + tiles
        + biases,
        [stack, stack, flat, flat, pltpu.VMEM((tokens, heads * columns), jnp.float32), flat],
    )
    return result.reshape(rows, columns, channels)


def solution(mesh):
    return jax.shard_map(
        shards,
        mesh=mesh,
        in_specs=(
            P(("crop", "row"), "col", None),
            P("crop"),
            P("crop", None),
            P(),
            P(),
            P(),
            P(),
            P(),
            P(),
            P(),
            P(),
            P(),
            P(),
        ),
        out_specs=P(("crop", "row"), "col", None),
        check_vma=False,
    )
```

```python
import functools
import math

import jax
import jax.numpy as jnp
from jax import lax
from jax.experimental import pallas as pl
from jax.experimental.pallas import tpu as pltpu
from jax.sharding import PartitionSpec as P

norm_epsilon = 1e-05
VMEM = pl.BlockSpec(memory_space=pltpu.VMEM)
PARAMS = pltpu.CompilerParams(vmem_limit_bytes=48 * 1024 * 1024)


def layer_norm(inputs, gain):
    average = jnp.mean(inputs, axis=-1, keepdims=True)
    centered = inputs - average
    variance = jnp.mean(centered * centered, axis=-1, keepdims=True)
    return centered * lax.rsqrt(variance + norm_epsilon) * gain


def dot(left, right):
    return jnp.dot(left, right, preferred_element_type=jnp.float32)


def pair_mask(row_mask, column_mask, rows, columns, row_start, column_start):
    along_rows = row_mask[pl.ds(row_start, rows)]
    along_columns = column_mask[pl.ds(pl.multiple_of(column_start, 8), columns), :]
    return (along_rows * along_columns[None]).reshape(rows * columns, -1)


def right_factor(rows, columns, step, normed, row_mask, column_mask, w_in):
    channels = normed.shape[1]
    row_start = lax.bitwise_xor(lax.axis_index("row"), step) * rows
    mask = pair_mask(row_mask, column_mask, rows, columns, row_start, lax.axis_index("col") * columns)
    part = dot(normed, w_in[:, 2 * channels :])
    value = mask * jax.nn.sigmoid(part[:, :channels]) * part[:, channels:]
    return value.astype(jnp.bfloat16).astype(jnp.float32)


def multiply(rows, columns, left, right, base, out, out_base):
    channels = left.shape[1]
    group = 4 if rows % 4 == 0 else 2
    for at in range(rows // group):
        sums = [jnp.zeros((columns, channels), jnp.float32) for _ in range(group)]
        for k in range(columns):
            factor = right[pl.ds(base + k, columns, stride=columns), :]
            for g in range(group):
                row = left[pl.ds((at * group + g) * columns + k, 1), :]
                sums[g] = sums[g] + row * factor
        width = group * columns
        out[pl.ds(out_base + at * width, width), :] = jnp.concatenate(sums, 0).astype(jnp.bfloat16)


def own_kernel(rows, columns, state, row_mask, column_mask, gain, w_in, w_gate, *refs):
    count = (len(refs) - 4) // 2
    weights, (left, gate, part_out), copies, right = refs[:count], refs[count : count + 3], refs[count + 3 : -1], refs[-1]
    channels = state.shape[1]
    size = rows * columns
    row_start = lax.axis_index("row") * rows
    column_start = lax.axis_index("col") * columns
    normed = layer_norm(state[...].astype(jnp.float32), gain[...]).astype(jnp.bfloat16)
    mask = pair_mask(row_mask, column_mask, rows, columns, row_start, column_start)
    part = dot(normed, w_in[:, : 2 * channels])
    value = mask * jax.nn.sigmoid(part[:, :channels]) * part[:, channels:]
    left[...] = value.astype(jnp.bfloat16).astype(jnp.float32)
    right[...] = right_factor(rows, columns, 0, normed, row_mask, column_mask, w_in)
    gate[...] = jax.nn.sigmoid(dot(normed, w_gate[...]))
    for part in range(rows // columns):
        multiply(rows, columns, left, right, part * columns * columns, part_out, part * size)
    for weight, copy in zip(weights, copies):
        copy[...] = weight[...]


def early_kernel(rows, columns, steps, row_mask, column_mask, gain, w_in, left, *refs):
    states, part_out, right = refs[: len(steps)], refs[-2], refs[-1]
    size = rows * columns
    split = rows // columns
    for at, (step, state) in enumerate(zip(steps, states)):
        normed = layer_norm(state[...].astype(jnp.float32), gain[...]).astype(jnp.bfloat16)
        right[...] = right_factor(rows, columns, step, normed, row_mask, column_mask, w_in)
        for part in range(split):
            multiply(rows, columns, left, right, part * columns * columns, part_out, (at * split + part) * size)


def late_kernel(rows, columns, steps, column_devices, row_mask, column_mask, gain, w_in, left, own, early, *refs):
    states, refs = refs[: len(steps)], refs[len(steps) :]
    outs, late, right = refs[:column_devices], refs[column_devices], refs[column_devices + 1]
    size = rows * columns
    split = rows // columns
    early_kernel(rows, columns, steps, row_mask, column_mask, gain, w_in, left, *states, late, right)
    row_index, column_index = lax.axis_index("row"), lax.axis_index("col")
    for step, out in enumerate(outs):
        target = lax.bitwise_xor(column_index, step)
        place = lax.bitwise_xor(row_index, target // split) * split + target % split

        def fill(source, first, last, out=out, place=place):
            @pl.when((place >= first) & (place < last))
            def _():
                out[...] = source[pl.ds(pl.multiple_of((place - first) * size, 16), size), :]

        fill(own, 0, split)
        fill(early, split, steps[0] * split)
        fill(late, steps[0] * split, (steps[-1] + 1) * split)


def middle_kernel(rows, columns, split, state, gate, product_gain, w_out, attend_gain, w_bias, *refs):
    parts, (middle, attend, bias) = refs[:-3], refs[-3:]
    product = parts[0][...].astype(jnp.float32)
    for part in parts[1:]:
        product = product + part[...].astype(jnp.float32)
    normed = layer_norm(product, product_gain[...]).astype(jnp.bfloat16)
    value = state[...].astype(jnp.float32) + gate[...] * dot(normed, w_out[...])
    rounded = value.astype(jnp.bfloat16)
    middle[...] = rounded
    normed = layer_norm(rounded.astype(jnp.float32), attend_gain[...]).astype(jnp.bfloat16)
    attend[...] = normed
    spread = dot(normed, w_bias[...]).reshape(rows, columns, -1)
    lane = lax.broadcasted_iota(jnp.int32, spread.shape[1:], 1) % columns
    for part in range(split):
        total = jnp.zeros(spread.shape[1:], jnp.float32)
        for j in range(columns):
            total = jnp.where(lane == j, spread[part * columns + j], total)
        bias[part] = total.astype(jnp.bfloat16)


def attend_kernel(rows, columns, heads, split, column_devices, middle, allowed, w_inputs, w_gate, w_out, *refs):
    tiles, refs = refs[:column_devices], refs[column_devices:]
    biases, refs = refs[:column_devices], refs[column_devices:]
    out, keys, values, queries, gates, bias, gated = refs
    channels = middle.shape[1]
    width = channels // heads
    tokens = columns * column_devices
    row_index, column_index = lax.axis_index("row"), lax.axis_index("col")
    for step, tile in enumerate(tiles):
        part = dot(tile[...], w_inputs[:, channels:]).reshape(rows, columns, 2 * channels)
        keys[:, pl.ds(step * columns, columns), :] = part[..., :channels]
        values[:, pl.ds(step * columns, columns), :] = part[..., channels:]
    own = tiles[0][...]
    queries[...] = dot(own, w_inputs[:, :channels])
    gates[...] = jax.nn.sigmoid(dot(own, w_gate[...]))
    for step, piece in enumerate(biases):
        place = lax.bitwise_xor(row_index * split + column_index % split, step)
        place = lax.bitwise_xor(place, column_index)
        bias[pl.ds(pl.multiple_of(place * columns, 8), columns), :] = piece[...].astype(jnp.float32)
    for step in range(column_devices):
        start = pl.multiple_of(lax.bitwise_xor(column_index, step) * columns, 8)
        here = pl.ds(step * columns, columns)
        bias[here, :] = jnp.where(allowed[pl.ds(start, columns), :] > 0, bias[here, :], -1e30)
    added = bias[...].T
    head_of_lane = (lax.broadcasted_iota(jnp.int32, (1, 2 * channels), 1) % channels) // width
    picks = [head_of_lane == h for h in range(heads)]
    scale = 1.0 / math.sqrt(width)
    ones = jnp.ones((tokens, channels), jnp.bfloat16)

    group = max(1, min(rows, 2304 // tokens))
    while rows % group:
        group -= 1

    def several(first, carry):
        places = [first * group + g for g in range(group)]
        starts = [pl.multiple_of(at * columns, 8) for at in places]
        scores = []
        for at, start in zip(places, starts):
            query = queries[pl.ds(start, columns), :]
            stacked = jnp.concatenate([jnp.where(pick[:, :channels], query, 0.0) for pick in picks], 0).astype(jnp.bfloat16)
            key = keys[at].astype(jnp.bfloat16)
            scores.append(lax.dot_general(stacked, key, (((1,), (1,)), ((), ())), preferred_element_type=jnp.float32))
        scores = [score * scale + added for score in scores]
        tops = [jnp.max(score, axis=-1, keepdims=True) for score in scores]
        weights = [jnp.exp(score - top).astype(jnp.bfloat16) for score, top in zip(scores, tops)]
        mixed = [
            dot(weight, jnp.concatenate([values[at].astype(jnp.bfloat16), ones], 1))
            for weight, at in zip(weights, places)
        ]
        for mix, start in zip(mixed, starts):
            total = mix[:columns]
            for h in range(1, heads):
                total = jnp.where(picks[h], mix[h * columns : (h + 1) * columns], total)
            here = pl.ds(start, columns)
            gated[here, :] = total[:, :channels] / total[:, channels:] * gates[here, :]
        return carry

    if group == rows:
        several(0, 0)
    else:
        lax.fori_loop(0, rows // group, several, 0)
    update = dot(gated[...].astype(jnp.bfloat16), w_out[...])
    out[...] = (middle[...].astype(jnp.float32) + update).astype(jnp.bfloat16)


def call(kernel, outs, args, scratch=()):
    return pl.pallas_call(
        kernel,
        out_shape=outs,
        in_specs=[VMEM] * len(args),
        out_specs=jax.tree.map(lambda _: VMEM, outs),
        scratch_shapes=scratch,
        compiler_params=PARAMS,
    )(*args)


def exchange(value, axis, step):
    size = lax.axis_size(axis)
    return lax.ppermute(value, axis, [(at, at ^ step) for at in range(size)])


def shards(
    pair_state,
    token_mask,
    block_pattern,
    triangle_norm,
    triangle_input,
    triangle_gate,
    product_norm,
    triangle_output,
    attend_norm,
    attend_inputs,
    attend_gate,
    attend_bias,
    attend_output,
):
    rows, columns, channels = pair_state.shape
    row_devices, column_devices = lax.axis_size("row"), lax.axis_size("col")
    heads = attend_bias.shape[1]
    split = rows // columns
    tokens = columns * column_devices
    size = rows * columns
    row_index, column_index = lax.axis_index("row"), lax.axis_index("col")
    tile = jax.ShapeDtypeStruct((size, channels), jnp.bfloat16)
    wide = jax.ShapeDtypeStruct((size, channels), jnp.float32)
    state = pair_state.reshape(size, channels)
    others = [exchange(state, "row", step) for step in range(1, row_devices)]

    valid = token_mask.astype(jnp.float32)
    row_mask = jnp.broadcast_to(valid[:, None, None], (tokens, 1, channels))
    column_mask = jnp.broadcast_to(valid[:, None], (tokens, channels))
    blocks = block_pattern.shape[0]
    block_width = tokens // blocks
    pattern = jnp.repeat(jnp.repeat(block_pattern, block_width, axis=0), block_width, axis=1)
    pattern = lax.dynamic_slice_in_dim(pattern, column_index * columns, columns, axis=0)
    allowed = ((pattern > 0) & (token_mask[None, :] > 0)).astype(jnp.float32).T
    allowed = jnp.tile(allowed, (1, heads))
    w_bias = jnp.repeat(attend_bias, columns, axis=1)

    norm_in = triangle_norm[None]
    weights = [
        product_norm[None],
        triangle_output,
        attend_norm[None],
        w_bias,
        allowed,
        attend_inputs,
        attend_gate,
        attend_output,
    ]
    flat = pltpu.VMEM((size, channels), jnp.float32)
    left, gate, own, *weights = call(
        functools.partial(own_kernel, rows, columns),
        [wide, wide, jax.ShapeDtypeStruct((split * size, channels), jnp.bfloat16)]
        + [jax.ShapeDtypeStruct(weight.shape, weight.dtype) for weight in weights],
        [state, row_mask, column_mask, norm_in, triangle_input, triangle_gate] + weights,
        [flat],
    )
    w_product, w_middle, w_attend, w_bias, allowed, w_inputs, w_gate, w_out = weights
    half = row_devices // 2
    early_steps, late_steps = list(range(1, half)), list(range(half, row_devices))
    common = [row_mask, column_mask, norm_in, triangle_input, left]
    early = call(
        functools.partial(early_kernel, rows, columns, early_steps),
        jax.ShapeDtypeStruct((len(early_steps) * split * size, channels), jnp.bfloat16),
        common + [others[step - 1] for step in early_steps],
        [flat],
    )
    parts = call(
        functools.partial(late_kernel, rows, columns, late_steps, column_devices),
        [tile] * column_devices,
        common + [own, early] + [others[step - 1] for step in late_steps],
        [pltpu.VMEM((len(late_steps) * split * size, channels), jnp.bfloat16), flat],
    )
    order = sorted(range(1, column_devices), key=lambda step: (step != 2, step))
    parts = [parts[0]] + [exchange(parts[step], "col", step) for step in order]
    middle, attend, bias = call(
        functools.partial(middle_kernel, rows, columns, split),
        [tile, tile, jax.ShapeDtypeStruct((split, columns, heads * columns), jnp.bfloat16)],
        [state, gate, w_product, w_middle, w_attend, w_bias] + parts,
    )
    moved = {step: exchange(attend, "col", step) for step in order}
    tiles = [attend] + [moved[step] for step in range(1, column_devices)]
    biases = []
    for step in range(column_devices):
        piece = bias[0]
        if split > 1:
            piece = lax.dynamic_index_in_dim(bias, lax.bitwise_xor(column_index, step) % split, 0, False)
        pairs = []
        for a in range(row_devices):
            for b in range(column_devices):
                turn = b ^ step
                pairs.append((a * column_devices + b, (turn // split) * column_devices + split * a + turn % split))
        biases.append(lax.ppermute(piece, ("row", "col"), pairs))
    stack = pltpu.VMEM((rows, tokens, channels), jnp.float32)
    result = call(
        functools.partial(attend_kernel, rows, columns, heads, split, column_devices),
        tile,
        [middle, allowed, w_inputs, w_gate, w_out]
        + tiles
        + biases,
        [stack, stack, flat, flat, pltpu.VMEM((tokens, heads * columns), jnp.float32), flat],
    )
    return result.reshape(rows, columns, channels)


def solution(mesh):
    return jax.shard_map(
        shards,
        mesh=mesh,
        in_specs=(
            P(("crop", "row"), "col", None),
            P("crop"),
            P("crop", None),
            P(),
            P(),
            P(),
            P(),
            P(),
            P(),
            P(),
            P(),
            P(),
            P(),
        ),
        out_specs=P(("crop", "row"), "col", None),
        check_vma=False,
    )
```

```python
import functools
import math

import jax
import jax.numpy as jnp
from jax import lax
from jax.experimental import pallas as pl
from jax.experimental.pallas import tpu as pltpu
from jax.sharding import PartitionSpec as P

norm_epsilon = 1e-05
VMEM = pl.BlockSpec(memory_space=pltpu.VMEM)
PARAMS = pltpu.CompilerParams(vmem_limit_bytes=48 * 1024 * 1024)


def layer_norm(inputs, gain):
    average = jnp.mean(inputs, axis=-1, keepdims=True)
    centered = inputs - average
    variance = jnp.mean(centered * centered, axis=-1, keepdims=True)
    return centered * lax.rsqrt(variance + norm_epsilon) * gain


def dot(left, right):
    return jnp.dot(left, right, preferred_element_type=jnp.float32)


def pair_mask(row_mask, column_mask, rows, columns, row_start, column_start):
    along_rows = row_mask[pl.ds(row_start, rows)]
    along_columns = column_mask[pl.ds(pl.multiple_of(column_start, 8), columns), :]
    return (along_rows * along_columns[None]).reshape(rows * columns, -1)


def right_factor(rows, columns, step, normed, row_mask, column_mask, w_in):
    channels = normed.shape[1]
    row_start = lax.bitwise_xor(lax.axis_index("row"), step) * rows
    mask = pair_mask(row_mask, column_mask, rows, columns, row_start, lax.axis_index("col") * columns)
    part = dot(normed, w_in[:, 2 * channels :])
    value = mask * jax.nn.sigmoid(part[:, :channels]) * part[:, channels:]
    return value.astype(jnp.bfloat16).astype(jnp.float32)


def multiply(rows, columns, left, right, base, out, out_base):
    channels = left.shape[1]
    group = 4 if rows % 4 == 0 else 2
    for at in range(rows // group):
        sums = [jnp.zeros((columns, channels), jnp.float32) for _ in range(group)]
        for k in range(columns):
            factor = right[pl.ds(base + k, columns, stride=columns), :]
            for g in range(group):
                row = left[pl.ds((at * group + g) * columns + k, 1), :]
                sums[g] = sums[g] + row * factor
        width = group * columns
        out[pl.ds(out_base + at * width, width), :] = jnp.concatenate(sums, 0).astype(jnp.bfloat16)


def own_kernel(rows, columns, state, row_mask, column_mask, gain, w_in, w_gate, *refs):
    count = (len(refs) - 4) // 2
    weights, (left, gate, part_out), copies, right = refs[:count], refs[count : count + 3], refs[count + 3 : -1], refs[-1]
    channels = state.shape[1]
    size = rows * columns
    row_start = lax.axis_index("row") * rows
    column_start = lax.axis_index("col") * columns
    normed = layer_norm(state[...].astype(jnp.float32), gain[...]).astype(jnp.bfloat16)
    mask = pair_mask(row_mask, column_mask, rows, columns, row_start, column_start)
    part = dot(normed, w_in[:, : 2 * channels])
    value = mask * jax.nn.sigmoid(part[:, :channels]) * part[:, channels:]
    left[...] = value.astype(jnp.bfloat16).astype(jnp.float32)
    right[...] = right_factor(rows, columns, 0, normed, row_mask, column_mask, w_in)
    gate[...] = jax.nn.sigmoid(dot(normed, w_gate[...]))
    for part in range(rows // columns):
        multiply(rows, columns, left, right, part * columns * columns, part_out, part * size)
    for weight, copy in zip(weights, copies):
        copy[...] = weight[...]


def early_kernel(rows, columns, steps, row_mask, column_mask, gain, w_in, left, *refs):
    states, part_out, right = refs[: len(steps)], refs[-2], refs[-1]
    size = rows * columns
    split = rows // columns
    for at, (step, state) in enumerate(zip(steps, states)):
        normed = layer_norm(state[...].astype(jnp.float32), gain[...]).astype(jnp.bfloat16)
        right[...] = right_factor(rows, columns, step, normed, row_mask, column_mask, w_in)
        for part in range(split):
            multiply(rows, columns, left, right, part * columns * columns, part_out, (at * split + part) * size)


def late_kernel(rows, columns, steps, column_devices, row_mask, column_mask, gain, w_in, left, own, early, *refs):
    states, refs = refs[: len(steps)], refs[len(steps) :]
    outs, late, right = refs[:column_devices], refs[column_devices], refs[column_devices + 1]
    size = rows * columns
    split = rows // columns
    early_kernel(rows, columns, steps, row_mask, column_mask, gain, w_in, left, *states, late, right)
    row_index, column_index = lax.axis_index("row"), lax.axis_index("col")
    for step, out in enumerate(outs):
        target = lax.bitwise_xor(column_index, step)
        place = lax.bitwise_xor(row_index, target // split) * split + target % split

        def fill(source, first, last, out=out, place=place):
            @pl.when((place >= first) & (place < last))
            def _():
                out[...] = source[pl.ds(pl.multiple_of((place - first) * size, 16), size), :]

        fill(own, 0, split)
        fill(late, split, (steps[-1] + 1) * split)
        fill(early, (steps[-1] + 1) * split, (steps[-1] + 1) * split + early.shape[0] // size)


def middle_kernel(rows, columns, split, state, gate, product_gain, w_out, attend_gain, w_bias, *refs):
    parts, (middle, attend, bias) = refs[:-3], refs[-3:]
    product = parts[0][...].astype(jnp.float32)
    for part in parts[1:]:
        product = product + part[...].astype(jnp.float32)
    normed = layer_norm(product, product_gain[...]).astype(jnp.bfloat16)
    value = state[...].astype(jnp.float32) + gate[...] * dot(normed, w_out[...])
    rounded = value.astype(jnp.bfloat16)
    middle[...] = rounded
    normed = layer_norm(rounded.astype(jnp.float32), attend_gain[...]).astype(jnp.bfloat16)
    attend[...] = normed
    for part, total in enumerate(bias_parts(rows, columns, split, normed, w_bias)):
        bias[part] = total.astype(jnp.bfloat16)


def bias_parts(rows, columns, split, normed, w_bias):
    spread = dot(normed, w_bias[...]).reshape(rows, columns, -1)
    lane = lax.broadcasted_iota(jnp.int32, spread.shape[1:], 1) % columns
    parts = []
    for part in range(split):
        total = jnp.zeros(spread.shape[1:], jnp.float32)
        for j in range(columns):
            total = jnp.where(lane == j, spread[part * columns + j], total)
        parts.append(total)
    return parts


def neighbor_kernel(rows, columns, split, own, attend, w_bias, bias):
    for part, total in enumerate(bias_parts(rows, columns, split, attend[...], w_bias)):
        bias[part] = jnp.concatenate([own[part].astype(jnp.float32), total], 0).astype(jnp.bfloat16)


def attend_kernel(rows, columns, heads, split, column_devices, arrival, middle, allowed, w_inputs, w_gate, w_out, *refs):
    tiles, refs = refs[:column_devices], refs[column_devices:]
    biases, refs = refs[: column_devices // 2], refs[column_devices // 2 :]
    out, keys, values, queries, gates, bias, gated = refs
    channels = middle.shape[1]
    width = channels // heads
    tokens = columns * column_devices
    row_index, column_index = lax.axis_index("row"), lax.axis_index("col")
    for step, tile in zip(arrival, tiles):
        part = dot(tile[...], w_inputs[:, channels:]).reshape(rows, columns, 2 * channels)
        keys[:, pl.ds(step * columns, columns), :] = part[..., :channels]
        values[:, pl.ds(step * columns, columns), :] = part[..., channels:]
    own = tiles[0][...]
    queries[...] = dot(own, w_inputs[:, :channels])
    gates[...] = jax.nn.sigmoid(dot(own, w_gate[...]))
    for step, piece in enumerate(biases):
        piece = piece[...].astype(jnp.float32)
        for side in range(2):
            place = lax.bitwise_xor(row_index * split + column_index % split, 2 * step + 1 - side)
            place = lax.bitwise_xor(place, column_index)
            here = pl.ds(pl.multiple_of(place * columns, 8), columns)
            bias[here, :] = piece[side * columns : (side + 1) * columns]
    for step in range(column_devices):
        start = pl.multiple_of(lax.bitwise_xor(column_index, step) * columns, 8)
        here = pl.ds(step * columns, columns)
        bias[here, :] = jnp.where(allowed[pl.ds(start, columns), :] > 0, bias[here, :], -1e30)
    added = bias[...].T
    head_of_lane = (lax.broadcasted_iota(jnp.int32, (1, 2 * channels), 1) % channels) // width
    picks = [head_of_lane == h for h in range(heads)]
    scale = 1.0 / math.sqrt(width)
    ones = jnp.ones((tokens, channels), jnp.bfloat16)

    group = max(1, min(rows, 2304 // tokens))
    while rows % group:
        group -= 1

    def several(first, carry):
        places = [first * group + g for g in range(group)]
        starts = [pl.multiple_of(at * columns, 8) for at in places]
        scores = []
        for at, start in zip(places, starts):
            query = queries[pl.ds(start, columns), :]
            stacked = jnp.concatenate([jnp.where(pick[:, :channels], query, 0.0) for pick in picks], 0).astype(jnp.bfloat16)
            key = keys[at].astype(jnp.bfloat16)
            scores.append(lax.dot_general(stacked, key, (((1,), (1,)), ((), ())), preferred_element_type=jnp.float32))
        scores = [score * scale + added for score in scores]
        tops = [jnp.max(score, axis=-1, keepdims=True) for score in scores]
        weights = [jnp.exp(score - top).astype(jnp.bfloat16) for score, top in zip(scores, tops)]
        mixed = [
            dot(weight, jnp.concatenate([values[at].astype(jnp.bfloat16), ones], 1))
            for weight, at in zip(weights, places)
        ]
        for mix, start in zip(mixed, starts):
            total = mix[:columns]
            for h in range(1, heads):
                total = jnp.where(picks[h], mix[h * columns : (h + 1) * columns], total)
            here = pl.ds(start, columns)
            gated[here, :] = total[:, :channels] / total[:, channels:] * gates[here, :]
        return carry

    if group == rows:
        several(0, 0)
    else:
        lax.fori_loop(0, rows // group, several, 0)
    update = dot(gated[...].astype(jnp.bfloat16), w_out[...])
    out[...] = (middle[...].astype(jnp.float32) + update).astype(jnp.bfloat16)


def call(kernel, outs, args, scratch=()):
    return pl.pallas_call(
        kernel,
        out_shape=outs,
        in_specs=[VMEM] * len(args),
        out_specs=jax.tree.map(lambda _: VMEM, outs),
        scratch_shapes=scratch,
        compiler_params=PARAMS,
    )(*args)


def exchange(value, axis, step):
    size = lax.axis_size(axis)
    return lax.ppermute(value, axis, [(at, at ^ step) for at in range(size)])


def shards(
    pair_state,
    token_mask,
    block_pattern,
    triangle_norm,
    triangle_input,
    triangle_gate,
    product_norm,
    triangle_output,
    attend_norm,
    attend_inputs,
    attend_gate,
    attend_bias,
    attend_output,
):
    rows, columns, channels = pair_state.shape
    row_devices, column_devices = lax.axis_size("row"), lax.axis_size("col")
    heads = attend_bias.shape[1]
    split = rows // columns
    tokens = columns * column_devices
    size = rows * columns
    row_index, column_index = lax.axis_index("row"), lax.axis_index("col")
    tile = jax.ShapeDtypeStruct((size, channels), jnp.bfloat16)
    wide = jax.ShapeDtypeStruct((size, channels), jnp.float32)
    state = pair_state.reshape(size, channels)
    others = [exchange(state, "row", step) for step in range(1, row_devices)]

    valid = token_mask.astype(jnp.float32)
    row_mask = jnp.broadcast_to(valid[:, None, None], (tokens, 1, channels))
    column_mask = jnp.broadcast_to(valid[:, None], (tokens, channels))
    blocks = block_pattern.shape[0]
    block_width = tokens // blocks
    pattern = jnp.repeat(jnp.repeat(block_pattern, block_width, axis=0), block_width, axis=1)
    pattern = lax.dynamic_slice_in_dim(pattern, column_index * columns, columns, axis=0)
    allowed = ((pattern > 0) & (token_mask[None, :] > 0)).astype(jnp.float32).T
    allowed = jnp.tile(allowed, (1, heads))
    w_bias = jnp.repeat(attend_bias, columns, axis=1)

    norm_in = triangle_norm[None]
    weights = [
        product_norm[None],
        triangle_output,
        attend_norm[None],
        w_bias,
        allowed,
        attend_inputs,
        attend_gate,
        attend_output,
    ]
    flat = pltpu.VMEM((size, channels), jnp.float32)
    left, gate, own, *weights = call(
        functools.partial(own_kernel, rows, columns),
        [wide, wide, jax.ShapeDtypeStruct((split * size, channels), jnp.bfloat16)]
        + [jax.ShapeDtypeStruct(weight.shape, weight.dtype) for weight in weights],
        [state, row_mask, column_mask, norm_in, triangle_input, triangle_gate] + weights,
        [flat],
    )
    w_product, w_middle, w_attend, w_bias, allowed, w_inputs, w_gate, w_out = weights
    early_steps = list(range(row_devices - row_devices // 4, row_devices))
    late_steps = list(range(1, early_steps[0]))
    common = [row_mask, column_mask, norm_in, triangle_input, left]
    early = call(
        functools.partial(early_kernel, rows, columns, early_steps),
        jax.ShapeDtypeStruct((len(early_steps) * split * size, channels), jnp.bfloat16),
        common + [others[step - 1] for step in early_steps],
        [flat],
    )
    parts = call(
        functools.partial(late_kernel, rows, columns, late_steps, column_devices),
        [tile] * column_devices,
        common + [own, early] + [others[step - 1] for step in late_steps],
        [pltpu.VMEM((len(late_steps) * split * size, channels), jnp.bfloat16), flat],
    )
    order = list(range(column_devices - 1, 2, -1)) + [1, 2]
    parts = [parts[0]] + [exchange(parts[step], "col", step) for step in order]
    middle, attend, bias = call(
        functools.partial(middle_kernel, rows, columns, split),
        [tile, tile, jax.ShapeDtypeStruct((split, columns, heads * columns), jnp.bfloat16)],
        [state, gate, w_product, w_middle, w_attend, w_bias] + parts,
    )
    moved = {step: exchange(attend, "col", step) for step in order}
    arrival = [0, 1] + list(range(column_devices - 1, 1, -1))
    tiles = [attend] + [moved[step] for step in arrival[1:]]
    both = call(
        functools.partial(neighbor_kernel, rows, columns, split),
        jax.ShapeDtypeStruct((split, 2 * columns, heads * columns), jnp.bfloat16),
        [bias, moved[1], w_bias],
    )
    biases = []
    for step in range(1, column_devices, 2):
        piece = both[0]
        if split > 1:
            piece = lax.dynamic_index_in_dim(both, lax.bitwise_xor(column_index, step) % split, 0, False)
        pairs = []
        for a in range(row_devices):
            for b in range(column_devices):
                turn = b ^ step
                pairs.append((a * column_devices + b, (turn // split) * column_devices + split * a + turn % split))
        biases.append(lax.ppermute(piece, ("row", "col"), pairs))
    stack = pltpu.VMEM((rows, tokens, channels), jnp.float32)
    result = call(
        functools.partial(attend_kernel, rows, columns, heads, split, column_devices, arrival),
        tile,
        [middle, allowed, w_inputs, w_gate, w_out]
        + tiles
        + biases,
        [stack, stack, flat, flat, pltpu.VMEM((tokens, heads * columns), jnp.float32), flat],
    )
    return result.reshape(rows, columns, channels)


def solution(mesh):
    return jax.shard_map(
        shards,
        mesh=mesh,
        in_specs=(
            P(("crop", "row"), "col", None),
            P("crop"),
            P("crop", None),
            P(),
            P(),
            P(),
            P(),
            P(),
            P(),
            P(),
            P(),
            P(),
            P(),
        ),
        out_specs=P(("crop", "row"), "col", None),
        check_vma=False,
    )
```

```python
import functools
import math

import jax
import jax.numpy as jnp
from jax import lax
from jax.experimental import pallas as pl
from jax.experimental.pallas import tpu as pltpu
from jax.sharding import PartitionSpec as P

norm_epsilon = 1e-05
VMEM = pl.BlockSpec(memory_space=pltpu.VMEM)


def layer_norm(inputs, gain):
    average = jnp.mean(inputs, axis=-1, keepdims=True)
    centered = inputs - average
    variance = jnp.mean(centered * centered, axis=-1, keepdims=True)
    return centered * lax.rsqrt(variance + norm_epsilon) * gain


def dot(left, right):
    return jnp.dot(left, right, preferred_element_type=jnp.float32)


def pair_mask(row_mask, column_mask, rows, columns, row_start, column_start):
    along_rows = row_mask[pl.ds(row_start, rows)]
    along_columns = column_mask[pl.ds(pl.multiple_of(column_start, 8), columns), :]
    return (along_rows * along_columns[None]).reshape(rows * columns, -1)


def right_factor(rows, columns, step, normed, row_mask, column_mask, w_in):
    channels = normed.shape[1]
    row_start = lax.bitwise_xor(lax.axis_index("row"), step) * rows
    mask = pair_mask(row_mask, column_mask, rows, columns, row_start, lax.axis_index("col") * columns)
    part = dot(normed, w_in[:, 2 * channels :])
    value = mask * jax.nn.sigmoid(part[:, :channels]) * part[:, channels:]
    return value.astype(jnp.bfloat16).astype(jnp.float32)


def multiply(rows, columns, left, right, base, out, out_base):
    channels = left.shape[1]
    group = 4 if rows % 4 == 0 else 2
    for at in range(rows // group):
        sums = [jnp.zeros((columns, channels), jnp.float32) for _ in range(group)]
        for k in range(columns):
            factor = right[pl.ds(base + k, columns, stride=columns), :]
            for g in range(group):
                row = left[pl.ds((at * group + g) * columns + k, 1), :]
                sums[g] = sums[g] + row * factor
        width = group * columns
        out[pl.ds(out_base + at * width, width), :] = jnp.concatenate(sums, 0).astype(jnp.bfloat16)


def own_kernel(rows, columns, state, row_mask, column_mask, gain, w_in, w_gate, *refs):
    count = (len(refs) - 4) // 2
    weights, (left, gate, part_out), copies, right = refs[:count], refs[count : count + 3], refs[count + 3 : -1], refs[-1]
    channels = state.shape[1]
    size = rows * columns
    row_start = lax.axis_index("row") * rows
    column_start = lax.axis_index("col") * columns
    normed = layer_norm(state[...].astype(jnp.float32), gain[...]).astype(jnp.bfloat16)
    mask = pair_mask(row_mask, column_mask, rows, columns, row_start, column_start)
    part = dot(normed, w_in[:, : 2 * channels])
    value = mask * jax.nn.sigmoid(part[:, :channels]) * part[:, channels:]
    left[...] = value.astype(jnp.bfloat16).astype(jnp.float32)
    right[...] = right_factor(rows, columns, 0, normed, row_mask, column_mask, w_in)
    gate[...] = jax.nn.sigmoid(dot(normed, w_gate[...]))
    for part in range(rows // columns):
        multiply(rows, columns, left, right, part * columns * columns, part_out, part * size)
    for weight, copy in zip(weights, copies):
        copy[...] = weight[...]


def early_kernel(rows, columns, steps, row_mask, column_mask, gain, w_in, left, *refs):
    states, part_out, right = refs[: len(steps)], refs[-2], refs[-1]
    size = rows * columns
    split = rows // columns
    for at, (step, state) in enumerate(zip(steps, states)):
        normed = layer_norm(state[...].astype(jnp.float32), gain[...]).astype(jnp.bfloat16)
        right[...] = right_factor(rows, columns, step, normed, row_mask, column_mask, w_in)
        for part in range(split):
            multiply(rows, columns, left, right, part * columns * columns, part_out, (at * split + part) * size)


def late_kernel(rows, columns, steps, column_devices, *refs):
    states, refs = refs[: len(steps)], refs[len(steps) :]
    row_mask, column_mask, gain, w_in, left, own, early, *refs = refs
    outs, late, right = refs[:column_devices], refs[column_devices], refs[column_devices + 1]
    size = rows * columns
    split = rows // columns
    early_kernel(rows, columns, steps, row_mask, column_mask, gain, w_in, left, *states, late, right)
    row_index, column_index = lax.axis_index("row"), lax.axis_index("col")
    for step, out in enumerate(outs):
        target = lax.bitwise_xor(column_index, step)
        place = lax.bitwise_xor(row_index, target // split) * split + target % split

        def fill(source, first, last, out=out, place=place):
            @pl.when((place >= first) & (place < last))
            def _():
                out[...] = source[pl.ds(pl.multiple_of((place - first) * size, 16), size), :]

        fill(own, 0, split)
        fill(late, split, (steps[-1] + 1) * split)
        fill(early, (steps[-1] + 1) * split, (steps[-1] + 1) * split + early.shape[0] // size)


def middle_kernel(rows, columns, split, state, gate, product_gain, w_out, attend_gain, w_bias, *refs):
    parts, (middle, attend, bias) = refs[:-3], refs[-3:]
    product = parts[0][...].astype(jnp.float32)
    for part in parts[1:]:
        product = product + part[...].astype(jnp.float32)
    normed = layer_norm(product, product_gain[...]).astype(jnp.bfloat16)
    value = state[...].astype(jnp.float32) + gate[...] * dot(normed, w_out[...])
    rounded = value.astype(jnp.bfloat16)
    middle[...] = rounded
    normed = layer_norm(rounded.astype(jnp.float32), attend_gain[...]).astype(jnp.bfloat16)
    attend[...] = normed
    for part, total in enumerate(bias_parts(rows, columns, split, normed, w_bias)):
        bias[part] = total.astype(jnp.bfloat16)


def bias_parts(rows, columns, split, normed, w_bias):
    spread = dot(normed, w_bias[...]).reshape(rows, columns, -1)
    lane = lax.broadcasted_iota(jnp.int32, spread.shape[1:], 1) % columns
    parts = []
    for part in range(split):
        total = jnp.zeros(spread.shape[1:], jnp.float32)
        for j in range(columns):
            total = jnp.where(lane == j, spread[part * columns + j], total)
        parts.append(total)
    return parts


def neighbor_kernel(rows, columns, split, own, attend, w_bias, bias):
    for part, total in enumerate(bias_parts(rows, columns, split, attend[...], w_bias)):
        bias[part] = jnp.concatenate([own[part].astype(jnp.float32), total], 0).astype(jnp.bfloat16)


def attend_kernel(rows, columns, heads, split, column_devices, arrival, middle, allowed, w_inputs, w_gate, w_out, *refs):
    tiles, refs = refs[:column_devices], refs[column_devices:]
    biases, refs = refs[: column_devices // 2], refs[column_devices // 2 :]
    out, keys, values, queries, gates, bias, gated = refs
    channels = middle.shape[1]
    width = channels // heads
    tokens = columns * column_devices
    row_index, column_index = lax.axis_index("row"), lax.axis_index("col")
    for step, tile in zip(arrival, tiles):
        part = dot(tile[...], w_inputs[:, channels:]).reshape(rows, columns, 2 * channels)
        keys[:, pl.ds(step * columns, columns), :] = part[..., :channels]
        values[:, pl.ds(step * columns, columns), :] = part[..., channels:]
    own = tiles[0][...]
    queries[...] = dot(own, w_inputs[:, :channels])
    gates[...] = jax.nn.sigmoid(dot(own, w_gate[...]))
    for step, piece in enumerate(biases):
        piece = piece[...].astype(jnp.float32)
        for side in range(2):
            place = lax.bitwise_xor(row_index * split + column_index % split, 2 * step + 1 - side)
            place = lax.bitwise_xor(place, column_index)
            here = pl.ds(pl.multiple_of(place * columns, 8), columns)
            bias[here, :] = piece[side * columns : (side + 1) * columns]
    for step in range(column_devices):
        start = pl.multiple_of(lax.bitwise_xor(column_index, step) * columns, 8)
        here = pl.ds(step * columns, columns)
        bias[here, :] = jnp.where(allowed[pl.ds(start, columns), :] > 0, bias[here, :], -1e30)
    added = bias[...].T
    head_of_lane = (lax.broadcasted_iota(jnp.int32, (1, 2 * channels), 1) % channels) // width
    picks = [head_of_lane == h for h in range(heads)]
    scale = 1.0 / math.sqrt(width)
    ones = jnp.ones((tokens, channels), jnp.bfloat16)

    group = max(1, min(rows, 2304 // tokens))
    while rows % group:
        group -= 1

    def several(first, carry):
        places = [first * group + g for g in range(group)]
        starts = [pl.multiple_of(at * columns, 8) for at in places]
        scores = []
        for at, start in zip(places, starts):
            query = queries[pl.ds(start, columns), :]
            stacked = jnp.concatenate([jnp.where(pick[:, :channels], query, 0.0) for pick in picks], 0).astype(jnp.bfloat16)
            key = keys[at].astype(jnp.bfloat16)
            scores.append(lax.dot_general(stacked, key, (((1,), (1,)), ((), ())), preferred_element_type=jnp.float32))
        scores = [score * scale + added for score in scores]
        tops = [jnp.max(score, axis=-1, keepdims=True) for score in scores]
        weights = [jnp.exp(score - top).astype(jnp.bfloat16) for score, top in zip(scores, tops)]
        mixed = [
            dot(weight, jnp.concatenate([values[at].astype(jnp.bfloat16), ones], 1))
            for weight, at in zip(weights, places)
        ]
        for mix, start in zip(mixed, starts):
            total = mix[:columns]
            for h in range(1, heads):
                total = jnp.where(picks[h], mix[h * columns : (h + 1) * columns], total)
            here = pl.ds(start, columns)
            gated[here, :] = total[:, :channels] / total[:, channels:] * gates[here, :]
        return carry

    if group == rows:
        several(0, 0)
    else:
        lax.fori_loop(0, rows // group, several, 0)
    update = dot(gated[...].astype(jnp.bfloat16), w_out[...])
    out[...] = (middle[...].astype(jnp.float32) + update).astype(jnp.bfloat16)


def call(kernel, outs, args, scratch=()):
    arrays = jax.tree.leaves(outs) + list(args) + list(scratch)
    held = sum(math.prod(array.shape) * jnp.dtype(array.dtype).itemsize for array in arrays)
    return pl.pallas_call(
        kernel,
        out_shape=outs,
        in_specs=[VMEM] * len(args),
        out_specs=jax.tree.map(lambda _: VMEM, outs),
        scratch_shapes=scratch,
        compiler_params=pltpu.CompilerParams(vmem_limit_bytes=min(56, 12 + 2 * held // 2**20) * 2**20),
    )(*args)


def exchange(value, axis, step):
    size = lax.axis_size(axis)
    return lax.ppermute(value, axis, [(at, at ^ step) for at in range(size)])


def shards(
    pair_state,
    token_mask,
    block_pattern,
    triangle_norm,
    triangle_input,
    triangle_gate,
    product_norm,
    triangle_output,
    attend_norm,
    attend_inputs,
    attend_gate,
    attend_bias,
    attend_output,
):
    rows, columns, channels = pair_state.shape
    row_devices, column_devices = lax.axis_size("row"), lax.axis_size("col")
    heads = attend_bias.shape[1]
    split = rows // columns
    tokens = columns * column_devices
    size = rows * columns
    row_index, column_index = lax.axis_index("row"), lax.axis_index("col")
    tile = jax.ShapeDtypeStruct((size, channels), jnp.bfloat16)
    wide = jax.ShapeDtypeStruct((size, channels), jnp.float32)
    state = pair_state.reshape(size, channels)
    others = [exchange(state, "row", step) for step in range(1, row_devices)]

    valid = token_mask.astype(jnp.float32)
    row_mask = jnp.broadcast_to(valid[:, None, None], (tokens, 1, channels))
    column_mask = jnp.broadcast_to(valid[:, None], (tokens, channels))
    blocks = block_pattern.shape[0]
    block_width = tokens // blocks
    pattern = jnp.repeat(jnp.repeat(block_pattern, block_width, axis=0), block_width, axis=1)
    pattern = lax.dynamic_slice_in_dim(pattern, column_index * columns, columns, axis=0)
    allowed = ((pattern > 0) & (token_mask[None, :] > 0)).astype(jnp.float32).T
    allowed = jnp.tile(allowed, (1, heads))
    w_bias = jnp.repeat(attend_bias, columns, axis=1)

    norm_in = triangle_norm[None]
    weights = [
        product_norm[None],
        triangle_output,
        attend_norm[None],
        w_bias,
        allowed,
        attend_inputs,
        attend_gate,
        attend_output,
    ]
    flat = pltpu.VMEM((size, channels), jnp.float32)
    left, gate, own, *weights = call(
        functools.partial(own_kernel, rows, columns),
        [wide, wide, jax.ShapeDtypeStruct((split * size, channels), jnp.bfloat16)]
        + [jax.ShapeDtypeStruct(weight.shape, weight.dtype) for weight in weights],
        [state, row_mask, column_mask, norm_in, triangle_input, triangle_gate] + weights,
        [flat],
    )
    w_product, w_middle, w_attend, w_bias, allowed, w_inputs, w_gate, w_out = weights
    early_steps = list(range(row_devices - row_devices // 4, row_devices))
    late_steps = list(range(1, early_steps[0]))
    common = [row_mask, column_mask, norm_in, triangle_input, left]
    early = call(
        functools.partial(early_kernel, rows, columns, early_steps),
        jax.ShapeDtypeStruct((len(early_steps) * split * size, channels), jnp.bfloat16),
        common + [others[step - 1] for step in early_steps],
        [flat],
    )
    parts = call(
        functools.partial(late_kernel, rows, columns, late_steps, column_devices),
        [tile] * column_devices,
        [others[step - 1] for step in late_steps] + common + [own, early],
        [pltpu.VMEM((len(late_steps) * split * size, channels), jnp.bfloat16), flat],
    )
    order = list(range(column_devices - 1, 2, -1)) + [1, 2]
    parts = [parts[0]] + [exchange(parts[step], "col", step) for step in order]
    middle, attend, bias = call(
        functools.partial(middle_kernel, rows, columns, split),
        [tile, tile, jax.ShapeDtypeStruct((split, columns, heads * columns), jnp.bfloat16)],
        [state, gate, w_product, w_middle, w_attend, w_bias] + parts,
    )
    moved = {step: exchange(attend, "col", step) for step in order}
    arrival = [0, 1] + list(range(column_devices - 1, 1, -1))
    tiles = [attend] + [moved[step] for step in arrival[1:]]
    both = call(
        functools.partial(neighbor_kernel, rows, columns, split),
        jax.ShapeDtypeStruct((split, 2 * columns, heads * columns), jnp.bfloat16),
        [bias, moved[1], w_bias],
    )
    biases = []
    for step in range(1, column_devices, 2):
        piece = both[0]
        if split > 1:
            piece = lax.dynamic_index_in_dim(both, lax.bitwise_xor(column_index, step) % split, 0, False)
        pairs = []
        for a in range(row_devices):
            for b in range(column_devices):
                turn = b ^ step
                pairs.append((a * column_devices + b, (turn // split) * column_devices + split * a + turn % split))
        biases.append(lax.ppermute(piece, ("row", "col"), pairs))
    stack = pltpu.VMEM((rows, tokens, channels), jnp.float32)
    result = call(
        functools.partial(attend_kernel, rows, columns, heads, split, column_devices, arrival),
        tile,
        [middle, allowed, w_inputs, w_gate, w_out]
        + tiles
        + biases,
        [stack, stack, flat, flat, pltpu.VMEM((tokens, heads * columns), jnp.float32), flat],
    )
    return result.reshape(rows, columns, channels)


def solution(mesh):
    return jax.shard_map(
        shards,
        mesh=mesh,
        in_specs=(
            P(("crop", "row"), "col", None),
            P("crop"),
            P("crop", None),
            P(),
            P(),
            P(),
            P(),
            P(),
            P(),
            P(),
            P(),
            P(),
            P(),
        ),
        out_specs=P(("crop", "row"), "col", None),
        check_vma=False,
    )
```

```python
import functools
import math

import jax
import jax.numpy as jnp
from jax import lax
from jax.experimental import pallas as pl
from jax.experimental.pallas import tpu as pltpu
from jax.sharding import PartitionSpec as P

norm_epsilon = 1e-05
VMEM = pl.BlockSpec(memory_space=pltpu.VMEM)


def layer_norm(inputs, gain):
    average = jnp.mean(inputs, axis=-1, keepdims=True)
    centered = inputs - average
    variance = jnp.mean(centered * centered, axis=-1, keepdims=True)
    return centered * lax.rsqrt(variance + norm_epsilon) * gain


def dot(left, right):
    return jnp.dot(left, right, preferred_element_type=jnp.float32)


def pair_mask(row_mask, column_mask, rows, columns, row_start, column_start):
    along_rows = row_mask[pl.ds(row_start, rows)]
    along_columns = column_mask[pl.ds(pl.multiple_of(column_start, 8), columns), :]
    return (along_rows * along_columns[None]).reshape(rows * columns, -1)


def right_factor(rows, columns, step, normed, row_mask, column_mask, w_in):
    channels = normed.shape[1]
    row_start = lax.bitwise_xor(lax.axis_index("row"), step) * rows
    mask = pair_mask(row_mask, column_mask, rows, columns, row_start, lax.axis_index("col") * columns)
    part = dot(normed, w_in[:, 2 * channels :])
    value = mask * jax.nn.sigmoid(part[:, :channels]) * part[:, channels:]
    return value.astype(jnp.bfloat16).astype(jnp.float32)


def multiply(rows, columns, left, right, base, out, out_base):
    channels = left.shape[1]
    group = 4 if rows % 4 == 0 else 2
    for at in range(rows // group):
        sums = [jnp.zeros((columns, channels), jnp.float32) for _ in range(group)]
        for k in range(columns):
            factor = right[pl.ds(base + k, columns, stride=columns), :]
            for g in range(group):
                row = left[pl.ds((at * group + g) * columns + k, 1), :]
                sums[g] = sums[g] + row * factor
        width = group * columns
        out[pl.ds(out_base + at * width, width), :] = jnp.concatenate(sums, 0).astype(jnp.bfloat16)


def own_kernel(rows, columns, state, row_mask, column_mask, gain, w_in, w_gate, *refs):
    count = (len(refs) - 4) // 2
    weights, (left, gate, part_out), copies, right = refs[:count], refs[count : count + 3], refs[count + 3 : -1], refs[-1]
    channels = state.shape[1]
    size = rows * columns
    row_start = lax.axis_index("row") * rows
    column_start = lax.axis_index("col") * columns
    normed = layer_norm(state[...].astype(jnp.float32), gain[...]).astype(jnp.bfloat16)
    mask = pair_mask(row_mask, column_mask, rows, columns, row_start, column_start)
    part = dot(normed, w_in[:, : 2 * channels])
    value = mask * jax.nn.sigmoid(part[:, :channels]) * part[:, channels:]
    left[...] = value.astype(jnp.bfloat16).astype(jnp.float32)
    right[...] = right_factor(rows, columns, 0, normed, row_mask, column_mask, w_in)
    gate[...] = jax.nn.sigmoid(dot(normed, w_gate[...]))
    for part in range(rows // columns):
        multiply(rows, columns, left, right, part * columns * columns, part_out, part * size)
    for weight, copy in zip(weights, copies):
        copy[...] = weight[...]


def early_kernel(rows, columns, steps, row_mask, column_mask, gain, w_in, left, *refs):
    states, part_out, right = refs[: len(steps)], refs[-2], refs[-1]
    size = rows * columns
    split = rows // columns
    for at, (step, state) in enumerate(zip(steps, states)):
        normed = layer_norm(state[...].astype(jnp.float32), gain[...]).astype(jnp.bfloat16)
        right[...] = right_factor(rows, columns, step, normed, row_mask, column_mask, w_in)
        for part in range(split):
            multiply(rows, columns, left, right, part * columns * columns, part_out, (at * split + part) * size)


def late_kernel(rows, columns, steps, column_devices, early_groups, *refs):
    states, refs = refs[: len(steps)], refs[len(steps) :]
    row_mask, column_mask, gain, w_in, left, own, *refs = refs
    early, refs = refs[: len(early_groups)], refs[len(early_groups) :]
    outs, late, right = refs[:column_devices], refs[column_devices], refs[column_devices + 1]
    size = rows * columns
    split = rows // columns
    early_kernel(rows, columns, steps, row_mask, column_mask, gain, w_in, left, *states, late, right)
    row_index, column_index = lax.axis_index("row"), lax.axis_index("col")
    for step, out in enumerate(outs):
        target = lax.bitwise_xor(column_index, step)
        place = lax.bitwise_xor(row_index, target // split) * split + target % split

        def fill(source, first, last, out=out, place=place):
            @pl.when((place >= first) & (place < last))
            def _():
                out[...] = source[pl.ds(pl.multiple_of((place - first) * size, 16), size), :]

        fill(own, 0, split)
        for group, source in zip(early_groups, early):
            fill(source, group[0] * split, (group[-1] + 1) * split)
        fill(late, steps[0] * split, (steps[-1] + 1) * split)


def middle_kernel(rows, columns, split, state, gate, product_gain, w_out, attend_gain, w_bias, *refs):
    parts, (middle, attend, bias) = refs[:-3], refs[-3:]
    product = parts[0][...].astype(jnp.float32)
    for part in parts[1:]:
        product = product + part[...].astype(jnp.float32)
    normed = layer_norm(product, product_gain[...]).astype(jnp.bfloat16)
    value = state[...].astype(jnp.float32) + gate[...] * dot(normed, w_out[...])
    rounded = value.astype(jnp.bfloat16)
    middle[...] = rounded
    normed = layer_norm(rounded.astype(jnp.float32), attend_gain[...]).astype(jnp.bfloat16)
    attend[...] = normed
    for part, total in enumerate(bias_parts(rows, columns, split, normed, w_bias)):
        bias[part] = total.astype(jnp.bfloat16)


def bias_parts(rows, columns, split, normed, w_bias):
    spread = dot(normed, w_bias[...]).reshape(rows, columns, -1)
    lane = lax.broadcasted_iota(jnp.int32, spread.shape[1:], 1) % columns
    parts = []
    for part in range(split):
        total = jnp.zeros(spread.shape[1:], jnp.float32)
        for j in range(columns):
            total = jnp.where(lane == j, spread[part * columns + j], total)
        parts.append(total)
    return parts


def neighbor_kernel(rows, columns, split, own, attend, w_bias, bias):
    for part, total in enumerate(bias_parts(rows, columns, split, attend[...], w_bias)):
        bias[part] = jnp.concatenate([own[part].astype(jnp.float32), total], 0).astype(jnp.bfloat16)


def attend_kernel(rows, columns, heads, split, column_devices, arrival, middle, allowed, w_inputs, w_gate, w_out, *refs):
    tiles, refs = refs[:column_devices], refs[column_devices:]
    biases, refs = refs[: column_devices // 2], refs[column_devices // 2 :]
    out, keys, values, queries, gates, bias, gated = refs
    channels = middle.shape[1]
    width = channels // heads
    tokens = columns * column_devices
    row_index, column_index = lax.axis_index("row"), lax.axis_index("col")
    for step, tile in zip(arrival, tiles):
        part = dot(tile[...], w_inputs[:, channels:]).reshape(rows, columns, 2 * channels)
        keys[:, pl.ds(step * columns, columns), :] = part[..., :channels]
        values[:, pl.ds(step * columns, columns), :] = part[..., channels:]
    own = tiles[0][...]
    queries[...] = dot(own, w_inputs[:, :channels])
    gates[...] = jax.nn.sigmoid(dot(own, w_gate[...]))
    for step, piece in enumerate(biases):
        piece = piece[...].astype(jnp.float32)
        for side in range(2):
            place = lax.bitwise_xor(row_index * split + column_index % split, 2 * step + 1 - side)
            place = lax.bitwise_xor(place, column_index)
            here = pl.ds(pl.multiple_of(place * columns, 8), columns)
            bias[here, :] = piece[side * columns : (side + 1) * columns]
    for step in range(column_devices):
        start = pl.multiple_of(lax.bitwise_xor(column_index, step) * columns, 8)
        here = pl.ds(step * columns, columns)
        bias[here, :] = jnp.where(allowed[pl.ds(start, columns), :] > 0, bias[here, :], -1e30)
    added = bias[...].T
    head_of_lane = (lax.broadcasted_iota(jnp.int32, (1, 2 * channels), 1) % channels) // width
    picks = [head_of_lane == h for h in range(heads)]
    scale = 1.0 / math.sqrt(width)
    ones = jnp.ones((tokens, channels), jnp.bfloat16)

    group = max(1, min(rows, 2304 // tokens))
    while rows % group:
        group -= 1

    def several(first, carry):
        places = [first * group + g for g in range(group)]
        starts = [pl.multiple_of(at * columns, 8) for at in places]
        scores = []
        for at, start in zip(places, starts):
            query = queries[pl.ds(start, columns), :]
            stacked = jnp.concatenate([jnp.where(pick[:, :channels], query, 0.0) for pick in picks], 0).astype(jnp.bfloat16)
            key = keys[at].astype(jnp.bfloat16)
            scores.append(lax.dot_general(stacked, key, (((1,), (1,)), ((), ())), preferred_element_type=jnp.float32))
        scores = [score * scale + added for score in scores]
        tops = [jnp.max(score, axis=-1, keepdims=True) for score in scores]
        weights = [jnp.exp(score - top).astype(jnp.bfloat16) for score, top in zip(scores, tops)]
        mixed = [
            dot(weight, jnp.concatenate([values[at].astype(jnp.bfloat16), ones], 1))
            for weight, at in zip(weights, places)
        ]
        for mix, start in zip(mixed, starts):
            total = mix[:columns]
            for h in range(1, heads):
                total = jnp.where(picks[h], mix[h * columns : (h + 1) * columns], total)
            here = pl.ds(start, columns)
            gated[here, :] = total[:, :channels] / total[:, channels:] * gates[here, :]
        return carry

    if group == rows:
        several(0, 0)
    else:
        lax.fori_loop(0, rows // group, several, 0)
    update = dot(gated[...].astype(jnp.bfloat16), w_out[...])
    out[...] = (middle[...].astype(jnp.float32) + update).astype(jnp.bfloat16)


def call(kernel, outs, args, scratch=()):
    arrays = jax.tree.leaves(outs) + list(args) + list(scratch)
    held = sum(math.prod(array.shape) * jnp.dtype(array.dtype).itemsize for array in arrays)
    return pl.pallas_call(
        kernel,
        out_shape=outs,
        in_specs=[VMEM] * len(args),
        out_specs=jax.tree.map(lambda _: VMEM, outs),
        scratch_shapes=scratch,
        compiler_params=pltpu.CompilerParams(vmem_limit_bytes=min(56, 12 + 2 * held // 2**20) * 2**20),
    )(*args)


def exchange(value, axis, step):
    size = lax.axis_size(axis)
    return lax.ppermute(value, axis, [(at, at ^ step) for at in range(size)])


def shards(
    pair_state,
    token_mask,
    block_pattern,
    triangle_norm,
    triangle_input,
    triangle_gate,
    product_norm,
    triangle_output,
    attend_norm,
    attend_inputs,
    attend_gate,
    attend_bias,
    attend_output,
):
    rows, columns, channels = pair_state.shape
    row_devices, column_devices = lax.axis_size("row"), lax.axis_size("col")
    heads = attend_bias.shape[1]
    split = rows // columns
    tokens = columns * column_devices
    size = rows * columns
    row_index, column_index = lax.axis_index("row"), lax.axis_index("col")
    tile = jax.ShapeDtypeStruct((size, channels), jnp.bfloat16)
    wide = jax.ShapeDtypeStruct((size, channels), jnp.float32)
    state = pair_state.reshape(size, channels)
    others = [exchange(state, "row", step) for step in range(1, row_devices)]

    valid = token_mask.astype(jnp.float32)
    row_mask = jnp.broadcast_to(valid[:, None, None], (tokens, 1, channels))
    column_mask = jnp.broadcast_to(valid[:, None], (tokens, channels))
    blocks = block_pattern.shape[0]
    block_width = tokens // blocks
    pattern = jnp.repeat(jnp.repeat(block_pattern, block_width, axis=0), block_width, axis=1)
    pattern = lax.dynamic_slice_in_dim(pattern, column_index * columns, columns, axis=0)
    allowed = ((pattern > 0) & (token_mask[None, :] > 0)).astype(jnp.float32).T
    allowed = jnp.tile(allowed, (1, heads))
    w_bias = jnp.repeat(attend_bias, columns, axis=1)

    norm_in = triangle_norm[None]
    weights = [
        product_norm[None],
        triangle_output,
        attend_norm[None],
        w_bias,
        allowed,
        attend_inputs,
        attend_gate,
        attend_output,
    ]
    flat = pltpu.VMEM((size, channels), jnp.float32)
    left, gate, own, *weights = call(
        functools.partial(own_kernel, rows, columns),
        [wide, wide, jax.ShapeDtypeStruct((split * size, channels), jnp.bfloat16)]
        + [jax.ShapeDtypeStruct(weight.shape, weight.dtype) for weight in weights],
        [state, row_mask, column_mask, norm_in, triangle_input, triangle_gate] + weights,
        [flat],
    )
    w_product, w_middle, w_attend, w_bias, allowed, w_inputs, w_gate, w_out = weights
    late_steps = list(range(row_devices - row_devices // 4, row_devices))
    early_steps = list(range(1, late_steps[0]))
    common = [row_mask, column_mask, norm_in, triangle_input, left]
    early_groups = [[step] for step in early_steps[::-1]]
    early = [
        call(
            functools.partial(early_kernel, rows, columns, group),
            jax.ShapeDtypeStruct((len(group) * split * size, channels), jnp.bfloat16),
            common + [others[step - 1] for step in group],
            [flat],
        )
        for group in early_groups
    ]
    parts = call(
        functools.partial(late_kernel, rows, columns, late_steps, column_devices, early_groups),
        [tile] * column_devices,
        [others[step - 1] for step in late_steps] + common + [own] + early,
        [pltpu.VMEM((len(late_steps) * split * size, channels), jnp.bfloat16), flat],
    )
    order = list(range(column_devices - 1, 2, -1)) + [1, 2]
    parts = [parts[0]] + [exchange(parts[step], "col", step) for step in order]
    middle, attend, bias = call(
        functools.partial(middle_kernel, rows, columns, split),
        [tile, tile, jax.ShapeDtypeStruct((split, columns, heads * columns), jnp.bfloat16)],
        [state, gate, w_product, w_middle, w_attend, w_bias] + parts,
    )
    moved = {step: exchange(attend, "col", step) for step in order}
    arrival = [0, 1] + list(range(column_devices - 1, 1, -1))
    tiles = [attend] + [moved[step] for step in arrival[1:]]
    both = call(
        functools.partial(neighbor_kernel, rows, columns, split),
        jax.ShapeDtypeStruct((split, 2 * columns, heads * columns), jnp.bfloat16),
        [bias, moved[1], w_bias],
    )
    biases = []
    for step in range(1, column_devices, 2):
        piece = both[0]
        if split > 1:
            piece = lax.dynamic_index_in_dim(both, lax.bitwise_xor(column_index, step) % split, 0, False)
        pairs = []
        for a in range(row_devices):
            for b in range(column_devices):
                turn = b ^ step
                pairs.append((a * column_devices + b, (turn // split) * column_devices + split * a + turn % split))
        biases.append(lax.ppermute(piece, ("row", "col"), pairs))
    stack = pltpu.VMEM((rows, tokens, channels), jnp.float32)
    result = call(
        functools.partial(attend_kernel, rows, columns, heads, split, column_devices, arrival),
        tile,
        [middle, allowed, w_inputs, w_gate, w_out]
        + tiles
        + biases,
        [stack, stack, flat, flat, pltpu.VMEM((tokens, heads * columns), jnp.float32), flat],
    )
    return result.reshape(rows, columns, channels)


def solution(mesh):
    return jax.shard_map(
        shards,
        mesh=mesh,
        in_specs=(
            P(("crop", "row"), "col", None),
            P("crop"),
            P("crop", None),
            P(),
            P(),
            P(),
            P(),
            P(),
            P(),
            P(),
            P(),
            P(),
            P(),
        ),
        out_specs=P(("crop", "row"), "col", None),
        check_vma=False,
    )
```

```python
import functools
import math

import jax
import jax.numpy as jnp
from jax import lax
from jax.experimental import pallas as pl
from jax.experimental.pallas import tpu as pltpu
from jax.sharding import PartitionSpec as P

norm_epsilon = 1e-05
VMEM = pl.BlockSpec(memory_space=pltpu.VMEM)


def layer_norm(inputs, gain):
    average = jnp.mean(inputs, axis=-1, keepdims=True)
    centered = inputs - average
    variance = jnp.mean(centered * centered, axis=-1, keepdims=True)
    return centered * lax.rsqrt(variance + norm_epsilon) * gain


def dot(left, right):
    return jnp.dot(left, right, preferred_element_type=jnp.float32)


def pair_mask(row_mask, column_mask, rows, columns, row_start, column_start):
    along_rows = row_mask[pl.ds(row_start, rows)]
    along_columns = column_mask[pl.ds(pl.multiple_of(column_start, 8), columns), :]
    return (along_rows * along_columns[None]).reshape(rows * columns, -1)


def right_factor(rows, columns, step, normed, row_mask, column_mask, w_in):
    channels = normed.shape[1]
    row_start = lax.bitwise_xor(lax.axis_index("row"), step) * rows
    mask = pair_mask(row_mask, column_mask, rows, columns, row_start, lax.axis_index("col") * columns)
    part = dot(normed, w_in[:, 2 * channels :])
    value = mask * jax.nn.sigmoid(part[:, :channels]) * part[:, channels:]
    return value.astype(jnp.bfloat16).astype(jnp.float32)


def multiply(rows, columns, left, right, base, out, out_base):
    channels = left.shape[1]
    group = 4 if rows % 4 == 0 else 2
    for at in range(rows // group):
        sums = [jnp.zeros((columns, channels), jnp.float32) for _ in range(group)]
        for k in range(columns):
            factor = right[pl.ds(base + k, columns, stride=columns), :]
            for g in range(group):
                row = left[pl.ds((at * group + g) * columns + k, 1), :]
                sums[g] = sums[g] + row * factor
        width = group * columns
        out[pl.ds(out_base + at * width, width), :] = jnp.concatenate(sums, 0).astype(jnp.bfloat16)


def own_kernel(rows, columns, state, row_mask, column_mask, gain, w_in, w_gate, *refs):
    count = (len(refs) - 4) // 2
    weights, (left, gate, part_out), copies, right = refs[:count], refs[count : count + 3], refs[count + 3 : -1], refs[-1]
    channels = state.shape[1]
    size = rows * columns
    row_start = lax.axis_index("row") * rows
    column_start = lax.axis_index("col") * columns
    normed = layer_norm(state[...].astype(jnp.float32), gain[...]).astype(jnp.bfloat16)
    mask = pair_mask(row_mask, column_mask, rows, columns, row_start, column_start)
    part = dot(normed, w_in[:, : 2 * channels])
    value = mask * jax.nn.sigmoid(part[:, :channels]) * part[:, channels:]
    left[...] = value.astype(jnp.bfloat16).astype(jnp.float32)
    right[pl.ds(0, size), :] = right_factor(rows, columns, 0, normed, row_mask, column_mask, w_in)
    gate[...] = jax.nn.sigmoid(dot(normed, w_gate[...]))
    for part in range(rows // columns):
        multiply(rows, columns, left, right, part * columns * columns, part_out, part * size)
    for weight, copy in zip(weights, copies):
        copy[...] = weight[...]


def early_kernel(rows, columns, steps, row_mask, column_mask, gain, w_in, left, *refs):
    states, part_out, right = refs[: len(steps)], refs[-2], refs[-1]
    size = rows * columns
    split = rows // columns
    for at, (step, state) in enumerate(zip(steps, states)):
        normed = layer_norm(state[...].astype(jnp.float32), gain[...]).astype(jnp.bfloat16)
        right[pl.ds(0, size), :] = right_factor(rows, columns, step, normed, row_mask, column_mask, w_in)
        for part in range(split):
            multiply(rows, columns, left, right, part * columns * columns, part_out, (at * split + part) * size)


def late_kernel(rows, columns, steps, column_devices, early_groups, *refs):
    states, refs = refs[: len(steps)], refs[len(steps) :]
    row_mask, column_mask, gain, w_in, left, own, *refs = refs
    early, refs = refs[: len(early_groups)], refs[len(early_groups) :]
    outs, late, right = refs[:column_devices], refs[column_devices], refs[column_devices + 1]
    size = rows * columns
    split = rows // columns
    early_kernel(rows, columns, steps, row_mask, column_mask, gain, w_in, left, *states, late, right)
    row_index, column_index = lax.axis_index("row"), lax.axis_index("col")
    for step, out in enumerate(outs):
        target = lax.bitwise_xor(column_index, step)
        place = lax.bitwise_xor(row_index, target // split) * split + target % split

        def fill(source, first, last, out=out, place=place):
            @pl.when((place >= first) & (place < last))
            def _():
                out[...] = source[pl.ds(pl.multiple_of((place - first) * size, 16), size), :]

        fill(own, 0, split)
        for group, source in zip(early_groups, early):
            fill(source, group[0] * split, (group[-1] + 1) * split)
        fill(late, steps[0] * split, (steps[-1] + 1) * split)


def middle_kernel(rows, columns, split, state, gate, product_gain, w_out, attend_gain, w_bias, *refs):
    parts, (middle, attend, bias) = refs[:-3], refs[-3:]
    product = parts[0][...].astype(jnp.float32)
    for part in parts[1:]:
        product = product + part[...].astype(jnp.float32)
    normed = layer_norm(product, product_gain[...]).astype(jnp.bfloat16)
    value = state[...].astype(jnp.float32) + gate[...] * dot(normed, w_out[...])
    rounded = value.astype(jnp.bfloat16)
    middle[...] = rounded
    normed = layer_norm(rounded.astype(jnp.float32), attend_gain[...]).astype(jnp.bfloat16)
    attend[...] = normed
    for part, total in enumerate(bias_parts(rows, columns, split, normed, w_bias)):
        bias[part] = total.astype(jnp.bfloat16)


def bias_parts(rows, columns, split, normed, w_bias):
    spread = dot(normed, w_bias[...]).reshape(rows, columns, -1)
    lane = lax.broadcasted_iota(jnp.int32, spread.shape[1:], 1) % columns
    parts = []
    for part in range(split):
        total = jnp.zeros(spread.shape[1:], jnp.float32)
        for j in range(columns):
            total = jnp.where(lane == j, spread[part * columns + j], total)
        parts.append(total)
    return parts


def neighbor_kernel(rows, columns, split, own, attend, w_bias, bias):
    for part, total in enumerate(bias_parts(rows, columns, split, attend[...], w_bias)):
        bias[part] = jnp.concatenate([own[part].astype(jnp.float32), total], 0).astype(jnp.bfloat16)


def project(rows, columns, w_inputs, tiles, keys, values):
    channels = w_inputs.shape[0]
    for at, tile in enumerate(tiles):
        part = dot(tile[...], w_inputs[:, channels:]).reshape(rows, columns, 2 * channels)
        here = pl.ds(at * columns, columns)
        keys[:, here, :] = part[..., :channels]
        values[:, here, :] = part[..., channels:]


def near_kernel(rows, columns, count, w_inputs, w_gate, *refs):
    tiles, (keys, values, queries, gates) = refs[:count], refs[count:]
    own = tiles[0][...]
    queries[...] = dot(own, w_inputs[:, : own.shape[1]])
    gates[...] = jax.nn.sigmoid(dot(own, w_gate[...]))
    project(rows, columns, w_inputs, tiles, keys, values)


def attend_kernel(rows, columns, heads, split, column_devices, arrival, middle, allowed, w_inputs, w_out, near_keys, near_values, queries, gates, *refs):
    far = len(arrival) - near_keys.shape[1] // columns
    tiles, refs = refs[:far], refs[far:]
    biases, refs = refs[: column_devices // 2], refs[column_devices // 2 :]
    out, far_keys, far_values, bias, gated = refs
    channels = middle.shape[1]
    width = channels // heads
    tokens = columns * column_devices
    row_index, column_index = lax.axis_index("row"), lax.axis_index("col")
    project(rows, columns, w_inputs, tiles, far_keys, far_values)
    for step, piece in enumerate(biases):
        piece = piece[...].astype(jnp.float32)
        for side in range(2):
            place = lax.bitwise_xor(row_index * split + column_index % split, 2 * step + 1 - side)
            place = lax.bitwise_xor(place, column_index)
            here = pl.ds(pl.multiple_of(place * columns, 8), columns)
            bias[here, :] = piece[side * columns : (side + 1) * columns]
    pieces = []
    for step in arrival:
        start = pl.multiple_of(lax.bitwise_xor(column_index, step) * columns, 8)
        piece = bias[pl.ds(step * columns, columns), :]
        pieces.append(jnp.where(allowed[pl.ds(start, columns), :] > 0, piece, -1e30))
    added = jnp.concatenate(pieces, 0).T
    head_of_lane = (lax.broadcasted_iota(jnp.int32, (1, 2 * channels), 1) % channels) // width
    picks = [head_of_lane == h for h in range(heads)]
    scale = 1.0 / math.sqrt(width)
    ones = jnp.ones((tokens, channels), jnp.bfloat16)

    group = max(1, min(rows, 2304 // tokens))
    while rows % group:
        group -= 1

    def several(first, carry):
        places = [first * group + g for g in range(group)]
        starts = [pl.multiple_of(at * columns, 8) for at in places]
        scores = []
        for at, start in zip(places, starts):
            query = queries[pl.ds(start, columns), :]
            stacked = jnp.concatenate([jnp.where(pick[:, :channels], query, 0.0) for pick in picks], 0).astype(jnp.bfloat16)
            key = jnp.concatenate([near_keys[at], far_keys[at]], 0).astype(jnp.bfloat16)
            scores.append(lax.dot_general(stacked, key, (((1,), (1,)), ((), ())), preferred_element_type=jnp.float32))
        scores = [score * scale + added for score in scores]
        tops = [jnp.max(score, axis=-1, keepdims=True) for score in scores]
        weights = [jnp.exp(score - top).astype(jnp.bfloat16) for score, top in zip(scores, tops)]
        held = [jnp.concatenate([near_values[at], far_values[at]], 0).astype(jnp.bfloat16) for at in places]
        mixed = [
            dot(weight, jnp.concatenate([value, ones], 1))
            for weight, value in zip(weights, held)
        ]
        for mix, start in zip(mixed, starts):
            total = mix[:columns]
            for h in range(1, heads):
                total = jnp.where(picks[h], mix[h * columns : (h + 1) * columns], total)
            here = pl.ds(start, columns)
            gated[here, :] = total[:, :channels] / total[:, channels:] * gates[here, :]
        return carry

    if group == rows:
        several(0, 0)
    else:
        lax.fori_loop(0, rows // group, several, 0)
    update = dot(gated[...].astype(jnp.bfloat16), w_out[...])
    out[...] = (middle[...].astype(jnp.float32) + update).astype(jnp.bfloat16)


def call(kernel, outs, args, scratch=()):
    arrays = jax.tree.leaves(outs) + list(args) + list(scratch)
    held = sum(math.prod(array.shape) * jnp.dtype(array.dtype).itemsize for array in arrays)
    return pl.pallas_call(
        kernel,
        out_shape=outs,
        in_specs=[VMEM] * len(args),
        out_specs=jax.tree.map(lambda _: VMEM, outs),
        scratch_shapes=scratch,
        compiler_params=pltpu.CompilerParams(vmem_limit_bytes=min(56, 12 + 2 * held // 2**20) * 2**20),
    )(*args)


def exchange(value, axis, step):
    size = lax.axis_size(axis)
    return lax.ppermute(value, axis, [(at, at ^ step) for at in range(size)])


def shards(
    pair_state,
    token_mask,
    block_pattern,
    triangle_norm,
    triangle_input,
    triangle_gate,
    product_norm,
    triangle_output,
    attend_norm,
    attend_inputs,
    attend_gate,
    attend_bias,
    attend_output,
):
    rows, columns, channels = pair_state.shape
    row_devices, column_devices = lax.axis_size("row"), lax.axis_size("col")
    heads = attend_bias.shape[1]
    split = rows // columns
    tokens = columns * column_devices
    size = rows * columns
    row_index, column_index = lax.axis_index("row"), lax.axis_index("col")
    tile = jax.ShapeDtypeStruct((size, channels), jnp.bfloat16)
    wide = jax.ShapeDtypeStruct((size, channels), jnp.float32)
    state = pair_state.reshape(size, channels)
    others = [exchange(state, "row", step) for step in range(1, row_devices)]

    valid = token_mask.astype(jnp.float32)
    row_mask = jnp.broadcast_to(valid[:, None, None], (tokens, 1, channels))
    column_mask = jnp.broadcast_to(valid[:, None], (tokens, channels))
    blocks = block_pattern.shape[0]
    block_width = tokens // blocks
    pattern = jnp.repeat(jnp.repeat(block_pattern, block_width, axis=0), block_width, axis=1)
    pattern = lax.dynamic_slice_in_dim(pattern, column_index * columns, columns, axis=0)
    allowed = ((pattern > 0) & (token_mask[None, :] > 0)).astype(jnp.float32).T
    allowed = jnp.tile(allowed, (1, heads))
    w_bias = jnp.repeat(attend_bias, columns, axis=1)

    norm_in = triangle_norm[None]
    weights = [
        product_norm[None],
        triangle_output,
        attend_norm[None],
        w_bias,
        allowed,
        attend_inputs,
        attend_gate,
        attend_output,
    ]
    flat = pltpu.VMEM((size, channels), jnp.float32)
    padded = pltpu.VMEM((size + columns, channels), jnp.float32)
    left, gate, own, *weights = call(
        functools.partial(own_kernel, rows, columns),
        [wide, wide, jax.ShapeDtypeStruct((split * size, channels), jnp.bfloat16)]
        + [jax.ShapeDtypeStruct(weight.shape, weight.dtype) for weight in weights],
        [state, row_mask, column_mask, norm_in, triangle_input, triangle_gate] + weights,
        [padded],
    )
    w_product, w_middle, w_attend, w_bias, allowed, w_inputs, w_gate, w_out = weights
    late_steps = list(range(row_devices - row_devices // 4, row_devices))
    early_steps = list(range(1, late_steps[0]))
    common = [row_mask, column_mask, norm_in, triangle_input, left]
    early_groups = [[step] for step in early_steps]
    early = [
        call(
            functools.partial(early_kernel, rows, columns, group),
            jax.ShapeDtypeStruct((len(group) * split * size, channels), jnp.bfloat16),
            common + [others[step - 1] for step in group],
            [padded],
        )
        for group in early_groups
    ]
    parts = call(
        functools.partial(late_kernel, rows, columns, late_steps, column_devices, early_groups),
        [tile] * column_devices,
        [others[step - 1] for step in late_steps] + common + [own] + early,
        [pltpu.VMEM((len(late_steps) * split * size, channels), jnp.bfloat16), padded],
    )
    order = list(range(column_devices - 1, 2, -1)) + [1, 2]
    parts = [parts[0]] + [exchange(parts[step], "col", step) for step in order]
    middle, attend, bias = call(
        functools.partial(middle_kernel, rows, columns, split),
        [tile, tile, jax.ShapeDtypeStruct((split, columns, heads * columns), jnp.bfloat16)],
        [state, gate, w_product, w_middle, w_attend, w_bias] + parts,
    )
    moved = {step: exchange(attend, "col", step) for step in order}
    arrival = list(range(column_devices))
    tiles = [attend] + [moved[step] for step in arrival[1:]]
    both = call(
        functools.partial(neighbor_kernel, rows, columns, split),
        jax.ShapeDtypeStruct((split, 2 * columns, heads * columns), jnp.bfloat16),
        [bias, moved[1], w_bias],
    )
    biases = []
    for step in range(1, column_devices, 2):
        piece = both[0]
        if split > 1:
            piece = lax.dynamic_index_in_dim(both, lax.bitwise_xor(column_index, step) % split, 0, False)
        pairs = []
        for a in range(row_devices):
            for b in range(column_devices):
                turn = b ^ step
                pairs.append((a * column_devices + b, (turn // split) * column_devices + split * a + turn % split))
        biases.append(lax.ppermute(piece, ("row", "col"), pairs))
    near = 2
    near_stack = jax.ShapeDtypeStruct((rows, near * columns, channels), jnp.float32)
    held = call(
        functools.partial(near_kernel, rows, columns, near),
        [near_stack, near_stack, wide, wide],
        [w_inputs, w_gate] + tiles[:near],
    )
    far_stack = pltpu.VMEM((rows, tokens - near * columns, channels), jnp.float32)
    result = call(
        functools.partial(attend_kernel, rows, columns, heads, split, column_devices, arrival),
        tile,
        [middle, allowed, w_inputs, w_out, *held] + tiles[near:] + biases,
        [far_stack, far_stack, pltpu.VMEM((tokens, heads * columns), jnp.float32), flat],
    )
    return result.reshape(rows, columns, channels)


def solution(mesh):
    return jax.shard_map(
        shards,
        mesh=mesh,
        in_specs=(
            P(("crop", "row"), "col", None),
            P("crop"),
            P("crop", None),
            P(),
            P(),
            P(),
            P(),
            P(),
            P(),
            P(),
            P(),
            P(),
            P(),
        ),
        out_specs=P(("crop", "row"), "col", None),
        check_vma=False,
    )
```

```python
import functools
import math

import jax
import jax.numpy as jnp
from jax import lax
from jax.experimental import pallas as pl
from jax.experimental.pallas import tpu as pltpu
from jax.sharding import PartitionSpec as P

norm_epsilon = 1e-05
VMEM = pl.BlockSpec(memory_space=pltpu.VMEM)


def layer_norm(inputs, gain):
    average = jnp.mean(inputs, axis=-1, keepdims=True)
    centered = inputs - average
    variance = jnp.mean(centered * centered, axis=-1, keepdims=True)
    return centered * lax.rsqrt(variance + norm_epsilon) * gain


def dot(left, right):
    return jnp.dot(left, right, preferred_element_type=jnp.float32)


def pair_mask(row_mask, column_mask, rows, columns, row_start, column_start):
    along_rows = row_mask[pl.ds(row_start, rows)]
    along_columns = column_mask[pl.ds(pl.multiple_of(column_start, 8), columns), :]
    return (along_rows * along_columns[None]).reshape(rows * columns, -1)


def right_factor(rows, columns, step, normed, row_mask, column_mask, w_in):
    channels = normed.shape[1]
    row_start = lax.bitwise_xor(lax.axis_index("row"), step) * rows
    mask = pair_mask(row_mask, column_mask, rows, columns, row_start, lax.axis_index("col") * columns)
    part = dot(normed, w_in[:, 2 * channels :])
    value = mask * jax.nn.sigmoid(part[:, :channels]) * part[:, channels:]
    return value.astype(jnp.bfloat16).astype(jnp.float32)


def multiply(rows, columns, left, right, base, out, out_base):
    channels = left.shape[1]
    group = 12 if rows % 12 == 0 else 2
    for at in range(rows // group):
        sums = [jnp.zeros((columns, channels), jnp.float32) for _ in range(group)]
        for k in range(columns):
            factor = right[pl.ds(base + k, columns, stride=columns), :]
            for g in range(group):
                row = left[pl.ds((at * group + g) * columns + k, 1), :]
                sums[g] = sums[g] + row * factor
        width = group * columns
        out[pl.ds(out_base + at * width, width), :] = jnp.concatenate(sums, 0).astype(jnp.bfloat16)


def own_kernel(rows, columns, state, row_mask, column_mask, gain, w_in, w_gate, *refs):
    count = (len(refs) - 4) // 2
    weights, (left, gate, part_out), copies, right = refs[:count], refs[count : count + 3], refs[count + 3 : -1], refs[-1]
    channels = state.shape[1]
    size = rows * columns
    row_start = lax.axis_index("row") * rows
    column_start = lax.axis_index("col") * columns
    normed = layer_norm(state[...].astype(jnp.float32), gain[...]).astype(jnp.bfloat16)
    mask = pair_mask(row_mask, column_mask, rows, columns, row_start, column_start)
    part = dot(normed, w_in[:, : 2 * channels])
    value = mask * jax.nn.sigmoid(part[:, :channels]) * part[:, channels:]
    left[...] = value.astype(jnp.bfloat16).astype(jnp.float32)
    right[pl.ds(0, size), :] = right_factor(rows, columns, 0, normed, row_mask, column_mask, w_in)
    gate[...] = jax.nn.sigmoid(dot(normed, w_gate[...]))
    for part in range(rows // columns):
        multiply(rows, columns, left, right, part * columns * columns, part_out, part * size)
    for weight, copy in zip(weights, copies):
        copy[...] = weight[...]


def early_kernel(rows, columns, steps, row_mask, column_mask, gain, w_in, left, *refs):
    states, part_out, right = refs[: len(steps)], refs[-2], refs[-1]
    size = rows * columns
    split = rows // columns
    for at, (step, state) in enumerate(zip(steps, states)):
        normed = layer_norm(state[...].astype(jnp.float32), gain[...]).astype(jnp.bfloat16)
        right[pl.ds(0, size), :] = right_factor(rows, columns, step, normed, row_mask, column_mask, w_in)
        for part in range(split):
            multiply(rows, columns, left, right, part * columns * columns, part_out, (at * split + part) * size)


def fill(columns, split, source, first, last, outs):
    section = outs[0].shape[0]
    row_index, column_index = lax.axis_index("row"), lax.axis_index("col")
    for step, out in enumerate(outs):
        target = lax.bitwise_xor(column_index, step)
        place = lax.bitwise_xor(row_index, target // split) * split + target % split

        @pl.when((place >= first) & (place < last))
        def _(out=out, place=place):
            out[...] = source[pl.ds(pl.multiple_of((place - first) * section, 16), section), :]


def place_kernel(columns, split, early_groups, own, *refs):
    early, outs = refs[: len(early_groups)], refs[len(early_groups) :]
    fill(columns, split, own, 0, split, outs)
    for group, source in zip(early_groups, early):
        fill(columns, split, source, group[0] * split, (group[-1] + 1) * split, outs)


def late_kernel(rows, columns, steps, column_devices, *refs):
    states, refs = refs[: len(steps)], refs[len(steps) :]
    row_mask, column_mask, gain, w_in, left, *refs = refs
    outs, late, right = refs[column_devices:-2], refs[-2], refs[-1]
    split = rows // columns
    early_kernel(rows, columns, steps, row_mask, column_mask, gain, w_in, left, *states, late, right)
    fill(columns, split, late, steps[0] * split, (steps[-1] + 1) * split, outs)


def middle_kernel(rows, columns, split, state, gate, product_gain, w_out, attend_gain, w_bias, *refs):
    parts, (middle, attend, bias) = refs[:-3], refs[-3:]
    product = parts[0][...].astype(jnp.float32)
    for part in parts[1:]:
        product = product + part[...].astype(jnp.float32)
    normed = layer_norm(product, product_gain[...]).astype(jnp.bfloat16)
    value = state[...].astype(jnp.float32) + gate[...] * dot(normed, w_out[...])
    rounded = value.astype(jnp.bfloat16)
    middle[...] = rounded
    normed = layer_norm(rounded.astype(jnp.float32), attend_gain[...]).astype(jnp.bfloat16)
    attend[...] = normed
    for part, total in enumerate(bias_parts(rows, columns, split, normed, w_bias)):
        bias[part] = total.astype(jnp.bfloat16)


def bias_parts(rows, columns, split, normed, w_bias):
    spread = dot(normed, w_bias[...]).reshape(rows, columns, -1)
    lane = lax.broadcasted_iota(jnp.int32, spread.shape[1:], 1) % columns
    parts = []
    for part in range(split):
        total = jnp.zeros(spread.shape[1:], jnp.float32)
        for j in range(columns):
            total = jnp.where(lane == j, spread[part * columns + j], total)
        parts.append(total)
    return parts


def neighbor_kernel(rows, columns, split, own, attend, w_bias, bias):
    for part, total in enumerate(bias_parts(rows, columns, split, attend[...], w_bias)):
        bias[part] = jnp.concatenate([own[part].astype(jnp.float32), total], 0).astype(jnp.bfloat16)


def project(rows, columns, w_inputs, tiles, keys, values):
    channels = w_inputs.shape[0]
    for at, tile in enumerate(tiles):
        part = dot(tile[...], w_inputs[:, channels:]).reshape(rows, columns, 2 * channels)
        here = pl.ds(at * columns, columns)
        keys[:, here, :] = part[..., :channels]
        values[:, here, :] = part[..., channels:]


def near_kernel(rows, columns, heads, count, w_inputs, w_gate, *refs):
    tiles, (keys, values, queries, gates) = refs[:count], refs[count:]
    own = tiles[0][...]
    channels = own.shape[1]
    gates[...] = jax.nn.sigmoid(dot(own, w_gate[...]))
    query = dot(own, w_inputs[:, :channels]).reshape(rows, columns, channels)
    head_of_lane = lax.broadcasted_iota(jnp.int32, (1, 1, channels), 2) // (channels // heads)
    queries[...] = jnp.concatenate([jnp.where(head_of_lane == h, query, 0.0) for h in range(heads)], 1).astype(jnp.bfloat16)
    parts = [dot(tile[...], w_inputs[:, channels:]).reshape(rows, columns, 2 * channels) for tile in tiles]
    both = jnp.concatenate(parts, 1).astype(jnp.bfloat16)
    keys[...] = both[..., :channels]
    values[...] = both[..., channels:]


def attend_kernel(rows, columns, heads, split, column_devices, arrival, middle, allowed, w_inputs, w_out, near_keys, near_values, queries, gates, *refs):
    far = len(arrival) - near_keys.shape[1] // columns
    tiles, refs = refs[:far], refs[far:]
    biases, refs = refs[: column_devices // 2], refs[column_devices // 2 :]
    out, far_keys, far_values, bias, gated = refs
    channels = middle.shape[1]
    width = channels // heads
    tokens = columns * column_devices
    row_index, column_index = lax.axis_index("row"), lax.axis_index("col")
    project(rows, columns, w_inputs, tiles, far_keys, far_values)
    for step, piece in enumerate(biases):
        piece = piece[...].astype(jnp.float32)
        for side in range(2):
            place = lax.bitwise_xor(row_index * split + column_index % split, 2 * step + 1 - side)
            place = lax.bitwise_xor(place, column_index)
            here = pl.ds(pl.multiple_of(place * columns, 8), columns)
            bias[here, :] = piece[side * columns : (side + 1) * columns]
    pieces = []
    for step in arrival:
        start = pl.multiple_of(lax.bitwise_xor(column_index, step) * columns, 8)
        piece = bias[pl.ds(step * columns, columns), :]
        pieces.append(jnp.where(allowed[pl.ds(start, columns), :] > 0, piece, -1e30))
    added = jnp.concatenate(pieces, 0).T
    head_of_lane = (lax.broadcasted_iota(jnp.int32, (1, 2 * channels), 1) % channels) // width
    picks = [head_of_lane == h for h in range(heads)]
    scale = 1.0 / math.sqrt(width)
    ones = jnp.ones((tokens, channels), jnp.bfloat16)

    group = max(1, min(rows, 2304 // tokens))
    while rows % group:
        group -= 1

    def several(first, carry):
        places = [first * group + g for g in range(group)]
        starts = [pl.multiple_of(at * columns, 8) for at in places]
        scores = []
        for at in places:
            key = jnp.concatenate([near_keys[at], far_keys[at].astype(jnp.bfloat16)], 0)
            scores.append(lax.dot_general(queries[at], key, (((1,), (1,)), ((), ())), preferred_element_type=jnp.float32))
        scores = [score * scale + added for score in scores]
        tops = [jnp.max(score, axis=-1, keepdims=True) for score in scores]
        weights = [jnp.exp(score - top).astype(jnp.bfloat16) for score, top in zip(scores, tops)]
        held = [jnp.concatenate([near_values[at], far_values[at].astype(jnp.bfloat16)], 0) for at in places]
        mixed = [
            dot(weight, jnp.concatenate([value, ones], 1))
            for weight, value in zip(weights, held)
        ]
        for mix, start in zip(mixed, starts):
            total = mix[:columns]
            for h in range(1, heads):
                total = jnp.where(picks[h], mix[h * columns : (h + 1) * columns], total)
            here = pl.ds(start, columns)
            gated[here, :] = total[:, :channels] / total[:, channels:] * gates[here, :]
        return carry

    if group == rows:
        several(0, 0)
    else:
        lax.fori_loop(0, rows // group, several, 0)
    update = dot(gated[...].astype(jnp.bfloat16), w_out[...])
    out[...] = (middle[...].astype(jnp.float32) + update).astype(jnp.bfloat16)


def call(kernel, outs, args, scratch=(), aliases=None):
    arrays = jax.tree.leaves(outs) + list(args) + list(scratch)
    held = sum(math.prod(array.shape) * jnp.dtype(array.dtype).itemsize for array in arrays)
    return pl.pallas_call(
        kernel,
        out_shape=outs,
        in_specs=[VMEM] * len(args),
        out_specs=jax.tree.map(lambda _: VMEM, outs),
        scratch_shapes=scratch,
        input_output_aliases=aliases or {},
        compiler_params=pltpu.CompilerParams(vmem_limit_bytes=min(56, 12 + 2 * held // 2**20) * 2**20),
    )(*args)


def exchange(value, axis, step):
    size = lax.axis_size(axis)
    return lax.ppermute(value, axis, [(at, at ^ step) for at in range(size)])


def shards(
    pair_state,
    token_mask,
    block_pattern,
    triangle_norm,
    triangle_input,
    triangle_gate,
    product_norm,
    triangle_output,
    attend_norm,
    attend_inputs,
    attend_gate,
    attend_bias,
    attend_output,
):
    rows, columns, channels = pair_state.shape
    row_devices, column_devices = lax.axis_size("row"), lax.axis_size("col")
    heads = attend_bias.shape[1]
    split = rows // columns
    tokens = columns * column_devices
    size = rows * columns
    row_index, column_index = lax.axis_index("row"), lax.axis_index("col")
    tile = jax.ShapeDtypeStruct((size, channels), jnp.bfloat16)
    wide = jax.ShapeDtypeStruct((size, channels), jnp.float32)
    state = pair_state.reshape(size, channels)
    others = [exchange(state, "row", step) for step in range(1, row_devices)]

    valid = token_mask.astype(jnp.float32)
    row_mask = jnp.broadcast_to(valid[:, None, None], (tokens, 1, channels))
    column_mask = jnp.broadcast_to(valid[:, None], (tokens, channels))
    blocks = block_pattern.shape[0]
    block_width = tokens // blocks
    pattern = jnp.repeat(jnp.repeat(block_pattern, block_width, axis=0), block_width, axis=1)
    pattern = lax.dynamic_slice_in_dim(pattern, column_index * columns, columns, axis=0)
    allowed = ((pattern > 0) & (token_mask[None, :] > 0)).astype(jnp.float32).T
    allowed = jnp.tile(allowed, (1, heads))
    w_bias = jnp.repeat(attend_bias, columns, axis=1)

    norm_in = triangle_norm[None]
    weights = [
        product_norm[None],
        triangle_output,
        attend_norm[None],
        w_bias,
        allowed,
        attend_inputs,
        attend_gate,
        attend_output,
    ]
    flat = pltpu.VMEM((size, channels), jnp.float32)
    padded = pltpu.VMEM((size + columns, channels), jnp.float32)
    left, gate, own, *weights = call(
        functools.partial(own_kernel, rows, columns),
        [wide, wide, jax.ShapeDtypeStruct((split * size, channels), jnp.bfloat16)]
        + [jax.ShapeDtypeStruct(weight.shape, weight.dtype) for weight in weights],
        [state, row_mask, column_mask, norm_in, triangle_input, triangle_gate] + weights,
        [padded],
    )
    w_product, w_middle, w_attend, w_bias, allowed, w_inputs, w_gate, w_out = weights
    late_steps = list(range(row_devices - row_devices // 4, row_devices))
    early_steps = list(range(1, late_steps[0]))
    common = [row_mask, column_mask, norm_in, triangle_input, left]
    early_groups = [[step] for step in early_steps]
    early = [
        call(
            functools.partial(early_kernel, rows, columns, group),
            jax.ShapeDtypeStruct((len(group) * split * size, channels), jnp.bfloat16),
            common + [others[step - 1] for step in group],
            [padded],
        )
        for group in early_groups
    ]
    placed = call(
        functools.partial(place_kernel, columns, split, early_groups),
        [tile] * column_devices,
        [own] + early,
    )
    late_states = [others[step - 1] for step in late_steps]
    start = len(late_states) + len(common)
    parts = call(
        functools.partial(late_kernel, rows, columns, late_steps, column_devices),
        [tile] * column_devices,
        late_states + common + list(placed),
        [pltpu.VMEM((len(late_steps) * split * size, channels), jnp.bfloat16), padded],
        {start + at: at for at in range(column_devices)},
    )
    order = list(range(column_devices - 1, 2, -1)) + [1, 2]
    parts = [parts[0]] + [exchange(parts[step], "col", step) for step in order]
    middle, attend, bias = call(
        functools.partial(middle_kernel, rows, columns, split),
        [tile, tile, jax.ShapeDtypeStruct((split, columns, heads * columns), jnp.bfloat16)],
        [state, gate, w_product, w_middle, w_attend, w_bias] + parts,
    )
    moved = {step: exchange(attend, "col", step) for step in order}
    arrival = list(range(column_devices))
    tiles = [attend] + [moved[step] for step in arrival[1:]]
    both = call(
        functools.partial(neighbor_kernel, rows, columns, split),
        jax.ShapeDtypeStruct((split, 2 * columns, heads * columns), jnp.bfloat16),
        [bias, moved[1], w_bias],
    )
    biases = []
    for step in range(1, column_devices, 2):
        piece = both[0]
        if split > 1:
            piece = lax.dynamic_index_in_dim(both, lax.bitwise_xor(column_index, step) % split, 0, False)
        pairs = []
        for a in range(row_devices):
            for b in range(column_devices):
                turn = b ^ step
                pairs.append((a * column_devices + b, (turn // split) * column_devices + split * a + turn % split))
        biases.append(lax.ppermute(piece, ("row", "col"), pairs))
    near = 2
    near_stack = jax.ShapeDtypeStruct((rows, near * columns, channels), jnp.bfloat16)
    held = call(
        functools.partial(near_kernel, rows, columns, heads, near),
        [near_stack, near_stack, jax.ShapeDtypeStruct((rows, heads * columns, channels), jnp.bfloat16), wide],
        [w_inputs, w_gate] + tiles[:near],
    )
    far_stack = pltpu.VMEM((rows, tokens - near * columns, channels), jnp.float32)
    result = call(
        functools.partial(attend_kernel, rows, columns, heads, split, column_devices, arrival),
        tile,
        [middle, allowed, w_inputs, w_out, *held] + tiles[near:] + biases,
        [far_stack, far_stack, pltpu.VMEM((tokens, heads * columns), jnp.float32), flat],
    )
    return result.reshape(rows, columns, channels)


def solution(mesh):
    return jax.shard_map(
        shards,
        mesh=mesh,
        in_specs=(
            P(("crop", "row"), "col", None),
            P("crop"),
            P("crop", None),
            P(),
            P(),
            P(),
            P(),
            P(),
            P(),
            P(),
            P(),
            P(),
            P(),
        ),
        out_specs=P(("crop", "row"), "col", None),
        check_vma=False,
    )
```
